128 devices in a mesh: dp: 16 (over z, x_lo, core), seq: 8 (over y, x_hi).
Axes of the slice: x: 4 (x_hi: 2, x_lo: 2; x = x_hi * 2 + x_lo), y: 4, z: 4, core: 2. Of those that a mesh axis runs over, the one named last changes fastest.
Arguments:
- inputs: float32 [16, 1024, 896], P('dp', 'seq'), may hold values from -6 to 6
- params: float32 [14925824], P(('dp', 'seq'))
- segments: int32 [16, 1024], P('dp'), may hold values from 0 to 1, as said below
- cotangent: float32 [16, 1024, 896], P('dp', 'seq'), may hold values from -6 to 6
Outputs:
- outputs: float32 [16, 1024, 896], P('dp', 'seq')
- input_grad: float32 [16, 1024, 896], P('dp', 'seq')
- param_grad: float32 [14925824], P(('dp', 'seq'))
The draws below stay inside these ranges and needn't reach their ends.
Inputs may be any that keep to these rules, and one draw needn't show every extreme that they name: `segments`: each row starts at 0 and rises by 0 or 1 from one position to the next; every document but a row's last holds 204 positions or more; in each group of 1 row that share an index of dp, one row drawn from the seed has a last document of 1 to 64 positions, its length drawn from the seed, after a first document that covers the rest.
All inputs are finite; a program needn't handle non-finite values.
Results may differ from the reference program's by a relative error of at most 0.012.
Values may be sent and summed in bfloat16 or wider, within the bound.
No kernel may reach another device: no remote copies, remote signals or barrier semaphores. Data moves between devices by JAX's collectives and lax.ppermute only.
A program may use at most 384 MiB of HBM per device.

```python
import math
import jax
import jax.numpy as jnp
from jax import lax

D = 896
FF = 4864
HEADS = 14
KV_HEADS = 2
HEAD_DIM = 64
SEQS = 1
LENGTH = 1024
SEQUENCES = 16
NPAD = 14925824


def draw_params(key, part):
    query_width = HEADS * HEAD_DIM
    key_width = KV_HEADS * HEAD_DIM
    sections = [(D, 0.1, 1.0), (D * query_width, D ** (-0.5), 0.0), (query_width, 0.3, 0.0), (D * key_width, D ** (-0.5), 0.0), (key_width, 0.3, 0.0), (D * key_width, D ** (-0.5), 0.0), (key_width, 0.05, 0.0), (query_width * D, 4.0 * query_width ** (-0.5), 0.0), (D, 0.1, 1.0), (D * FF, D ** (-0.5), 0.0), (D * FF, D ** (-0.5), 0.0), (FF * D, FF ** (-0.5), 0.0)]
    used_total = sum((entry[0] for entry in sections))
    sections.append((NPAD - used_total, 1.0, 0.0))
    scales = jnp.concatenate([jnp.full((entry[0],), entry[1], jnp.float32) for entry in sections])
    centers = jnp.concatenate([jnp.full((entry[0],), entry[2], jnp.float32) for entry in sections])
    base = jnp.clip(jax.random.normal(key, (NPAD,), jnp.float32), -4.0, 4.0)
    return centers + scales * base


def draw_segments(key, part):
    key_lengths = jax.random.fold_in(key, 11)
    key_pick = jax.random.fold_in(key, 23)
    key_tail = jax.random.fold_in(key, 37)
    doc_lengths = jax.random.randint(key_lengths, (SEQUENCES, 6), LENGTH // 5, 2 * LENGTH)
    doc_ends = jnp.cumsum(doc_lengths, axis=1)
    places = jnp.arange(LENGTH, dtype=jnp.int32)
    numbers = jnp.sum((places[None, :, None] >= doc_ends[:, None, :]).astype(jnp.int32), axis=-1)
    numbers = jnp.minimum(numbers, 1)
    groups = SEQUENCES // SEQS
    picked = jax.random.randint(key_pick, (groups,), 0, SEQS) + jnp.arange(groups, dtype=jnp.int32) * SEQS
    rows_all = jnp.arange(SEQUENCES, dtype=jnp.int32)
    spanning_row = jnp.any(rows_all[:, None] == picked[None, :], axis=1)
    tails = jax.random.randint(key_tail, (SEQUENCES,), 1, LENGTH // 16 + 1)
    spanning = (places[None, :] >= LENGTH - tails[:, None]).astype(jnp.int32)
    return jnp.where(spanning_row[:, None], spanning, numbers).astype(jnp.int32)


def level_of(stream_key, shape, cuts, low, top_value):
    def one(position, shards_of):
        heights = jax.random.uniform(jax.random.fold_in(jax.random.fold_in(stream_key, 6), position), (shards_of,), jnp.float32, low / len(cuts), top_value / len(cuts))
        return jnp.repeat(jnp.exp(heights), shape[position] // shards_of).reshape((-1,) + (1,) * (len(shape) - position - 1))

    factor_of = one(*cuts[0])
    for cut in cuts[1:]:
        factor_of = factor_of * one(*cut)
    return factor_of


def centred(stream_key, dims, spread, reach, cuts=(), kind=jnp.bfloat16):
    factor_of = level_of(stream_key, dims, cuts, -0.22, 0.18) if cuts else 1.0
    array = jax.random.normal(stream_key, dims, jnp.float32) * spread * factor_of
    return jnp.minimum(jnp.maximum(array, -reach), reach).astype(kind)


def setup_inputs(seed: int = 0) -> dict:
    seeds = jax.random.split(jax.random.key(seed), 5)
    return {
        "inputs": centred(seeds[0], (SEQUENCES, LENGTH, D), 1.0, 6.0, ((0, 16), (1, 8)), jnp.float32),
        "params": draw_params(jax.random.fold_in(seeds[4], 71), 0),
        "segments": draw_segments(jax.random.fold_in(seeds[4], 71), 0),
        "cotangent": centred(seeds[3], (SEQUENCES, LENGTH, D), 1.0, 6.0, ((0, 16), (1, 8)), jnp.float32),
    }


@jax.custom_vjp
def low(v):
    return lax.optimization_barrier(v.astype(jnp.bfloat16)).astype(jnp.float32)

@jax.custom_vjp
def low_back(v):
    return v

def low_keep(v):
    return (low(v), None)

def low_pass(kept, grad):
    return (grad,)

def back_keep(v):
    return (v, None)

def back_low(kept, grad):
    return (low(grad),)
low.defvjp(low_keep, low_pass)
low_back.defvjp(back_keep, back_low)
EPS = 1e-06
ROPE_BASE = 1000000.0
HIGHEST = lax.Precision.HIGHEST

def layout():
    query_width = HEADS * HEAD_DIM
    key_width = KV_HEADS * HEAD_DIM
    return [(D,), (D, query_width), (query_width,), (D, key_width), (key_width,), (D, key_width), (key_width,), (query_width, D), (D,), (D, FF), (D, FF), (FF, D)]

def unpack(flat_vector):
    pieces = []
    offset = 0
    for extent in layout():
        amount = math.prod(extent)
        pieces.append(flat_vector[offset:offset + amount].reshape(extent))
        offset = offset + amount
    return pieces

def doc_positions(segments):
    length_all = segments.shape[-1]
    places = jnp.broadcast_to(jnp.arange(length_all, dtype=jnp.int32), segments.shape)
    previous = jnp.concatenate([segments[..., :1] - 1, segments[..., :-1]], axis=-1)
    starts = jnp.where(segments != previous, places, 0)
    return places - lax.cummax(starts, axis=segments.ndim - 1)

def rope_tables(positions):
    half_dim = HEAD_DIM // 2
    freqs = ROPE_BASE ** (-(jnp.arange(half_dim, dtype=jnp.float32) * 2.0) / HEAD_DIM)
    angles = positions.astype(jnp.float32)[..., None] * freqs
    return (jnp.cos(angles), jnp.sin(angles))

def rotate(values, cosine, sine):
    half_dim = values.shape[-1] // 2
    first = values[..., :half_dim]
    second = values[..., half_dim:]
    return jnp.concatenate([first * cosine - second * sine, second * cosine + first * sine], axis=-1)

def layer_forward(token_rows, seg_row, weights):
    gain_one, query_w, query_b, key_w, key_b, value_w, value_b, out_w, gain_two, gate_w, up_w, down_w = weights
    length_all = token_rows.shape[0]
    group_size = HEADS // KV_HEADS
    recip_one = lax.rsqrt(lax.optimization_barrier(jnp.mean(token_rows * token_rows, axis=-1, keepdims=True)) + EPS)
    normed_one = low(token_rows * recip_one * gain_one)
    query_pre = low_back(jnp.dot(normed_one, query_w, precision=HIGHEST) + query_b)
    key_pre = low_back(jnp.dot(normed_one, key_w, precision=HIGHEST) + key_b)
    value_pre = low_back(jnp.dot(normed_one, value_w, precision=HIGHEST) + value_b)
    cosine, sine = rope_tables(doc_positions(seg_row))
    query_rot = low(rotate(query_pre.reshape(length_all, HEADS, HEAD_DIM), cosine[:, None], sine[:, None]))
    key_rot = low(rotate(key_pre.reshape(length_all, KV_HEADS, HEAD_DIM), cosine[:, None], sine[:, None]))
    value_low = low(value_pre).reshape(length_all, KV_HEADS, HEAD_DIM)
    query_grouped = query_rot.reshape(length_all, KV_HEADS, group_size, HEAD_DIM)
    scores = jnp.einsum('qhgd,khd->hgqk', query_grouped, key_rot, precision=HIGHEST) * HEAD_DIM ** (-0.5)
    scores = low_back(scores)
    places = jnp.arange(length_all, dtype=jnp.int32)
    allowed = (seg_row[:, None] == seg_row[None, :]) & (places[None, :] <= places[:, None])
    masked = jnp.where(allowed, scores, -1e+30)
    shares = low(jax.nn.softmax(masked, axis=-1))
    attended = jnp.einsum('hgqk,khd->qhgd', shares, value_low, precision=HIGHEST)
    attended = low_back(low(attended.reshape(length_all, HEADS * HEAD_DIM)))
    attn_out = low_back(jnp.dot(attended, out_w, precision=HIGHEST))
    residual_mid = token_rows + attn_out
    recip_two = lax.rsqrt(lax.optimization_barrier(jnp.mean(residual_mid * residual_mid, axis=-1, keepdims=True)) + EPS)
    normed_two = low(residual_mid * recip_two * gain_two)
    gate_pre = low_back(jnp.dot(normed_two, gate_w, precision=HIGHEST))
    up_pre = low_back(jnp.dot(normed_two, up_w, precision=HIGHEST))
    hidden = low(jax.nn.silu(gate_pre) * up_pre)
    mlp_out = low_back(jnp.dot(hidden, down_w, precision=HIGHEST))
    return residual_mid + mlp_out

def reference(inputs, params, segments, cotangent):

    def forward(inputs_all, params_all):
        weights = unpack(low(params_all))

        def per_sequence(pair_item):
            return layer_forward(pair_item[0], pair_item[1], weights)
        return lax.map(jax.checkpoint(per_sequence), (inputs_all, segments))
    outputs, pullback = jax.vjp(forward, inputs, params)
    input_grad, param_grad = pullback(cotangent)
    return (outputs, input_grad, param_grad)
```

```python
import functools

import jax
import jax.numpy as jnp
import numpy as np
from jax import lax
from jax.experimental import pallas as pl
from jax.experimental.pallas import tpu as pltpu
from jax.sharding import Mesh, PartitionSpec as P

D = 896
FF = 4864
HEADS = 14
KV_HEADS = 2
HEAD_DIM = 64
GROUP = HEADS // KV_HEADS
EPS = 1e-06
ROPE_BASE = 1000000.0
LANES = 128

CHUNK = 911
TILES = FF // LANES
WIDE = 40
SPAN = D // LANES
Q_ROWS = D * SPAN
GU_START = SPAN + Q_ROWS + SPAN + D + 1 + D + 1 + Q_ROWS + SPAN
GU_ROWS = 2 * D * TILES
DOWN_START = GU_START + GU_ROWS
DOWN_ROWS = FF * SPAN
ATTN_CHUNKS = 16
MEMBERS = 8
UNITS = 640
GU_WIN = 25
DOWN_WIN = 18
SLOTS = 128
DOWN_SLOT = 2
PARTS = 8
PART_ROWS = 120
GU_FIRST, GU_LAST = 15, 90
DOWN_FIRST = 90
MIX_GU = 13
MIX_SKIP = 9

BF = jnp.bfloat16
F32 = jnp.float32


def dot(left, right, dims):
    return lax.dot_general(left, right, (dims, ((), ())), preferred_element_type=F32)


def mm(left, right):
    return dot(left, right, ((1,), (0,)))


def mm_nt(left, right):
    return dot(left, right, ((1,), (1,)))


def mm_tn(left, right):
    return dot(left, right, ((0,), (0,)))


def swap(value, axis):
    return lax.ppermute(value, axis, [(0, 1), (1, 0)])


def xor(value, axis, step, size):
    return lax.ppermute(value, axis, [(i, i ^ step) for i in range(size)])


def gather_abs(value, axis, size):
    me = lax.axis_index(axis)
    out = jnp.zeros((size,) + value.shape, value.dtype)
    out = lax.dynamic_update_index_in_dim(out, value, me, 0)
    for step in range(1, size):
        out = lax.dynamic_update_index_in_dim(out, xor(value, axis, step, size), me ^ step, 0)
    return out


def scatter_sum(value, axis, size):
    me = lax.axis_index(axis)
    total = lax.dynamic_index_in_dim(value, me, 0, keepdims=False).astype(F32)
    for step in range(1, size):
        block = lax.dynamic_index_in_dim(value, me ^ step, 0, keepdims=False)
        total = total + xor(block, axis, step, size).astype(F32)
    return total


def gather_attention(rows):
    parts = jnp.pad(rows, ((0, PARTS * PART_ROWS - CHUNK), (0, 0))).reshape(PARTS, PART_ROWS, LANES)
    part = lax.all_to_all(parts, ("z", "xl"), 0, 0, tiled=True)[0]
    copies = jnp.broadcast_to(part[None], (8 * PARTS, PART_ROWS, LANES))
    own = lax.all_to_all(copies, ("y", "xh", "z", "xl"), 0, 0, tiled=True)
    own = own.reshape(8, PARTS * PART_ROWS, LANES)
    return own, swap(own, "c")


def scatter_attention(own, other):
    half = (own.astype(F32) + swap(other, "c").astype(F32)).astype(BF)
    half = half.reshape(8 * PARTS, PART_ROWS, LANES)
    half = lax.all_to_all(half, ("y", "xh", "z", "xl"), 0, 0, tiled=True)
    part = jnp.sum(half.astype(F32), axis=0).astype(BF)
    copies = jnp.broadcast_to(part[None], (PARTS, PART_ROWS, LANES))
    parts = lax.all_to_all(copies, ("z", "xl"), 0, 0, tiled=True)
    return parts.reshape(-1, LANES)[:CHUNK]


def lane_order():
    m = np.arange(8)[:, None]
    lane = np.arange(LANES)[None, :]
    target = (lane % MEMBERS) * LANES + m * 16 + lane // MEMBERS
    return jnp.asarray(target.reshape(-1), jnp.int32)


def lane_matrix():
    target = lane_order()
    return (target[:, None] == jnp.arange(1024, dtype=jnp.int32)[None, :]).astype(BF)


def chunk_places(chunk):
    base = chunk * CHUNK - GU_START
    first = base // TILES
    base_down = chunk * CHUNK - DOWN_START
    first_down = base_down // (MEMBERS * SPAN)
    local = jnp.arange(CHUNK, dtype=jnp.int32)[:, None]
    is_gu = (base + local >= 0) & (base + local < GU_ROWS)
    is_down = (base_down + local >= 0) & (base_down + local < DOWN_ROWS)
    return base - first * TILES, base_down - first_down * MEMBERS * SPAN, is_gu, is_down


def cut_chunk(rows, chunk):
    phase, phase_down, is_gu, is_down = chunk_places(chunk)
    window = jnp.pad(jnp.where(is_gu, rows, 0), ((TILES, TILES + 1), (0, 0)))
    window = lax.dynamic_slice_in_dim(window, TILES - phase, GU_WIN * TILES, 0)
    window = jnp.pad(window.reshape(GU_WIN, TILES, LANES), ((0, 0), (0, WIDE - TILES), (0, 0)))
    window = window.reshape(GU_WIN, 5, 8, LANES).transpose(1, 0, 2, 3).reshape(GU_WIN * 5, 8 * LANES)
    gu = mm(window, lane_matrix()).astype(BF)
    gu = gu.reshape(5, GU_WIN, MEMBERS, LANES).transpose(2, 0, 1, 3)
    group = MEMBERS * SPAN
    window = jnp.pad(jnp.where(is_down, rows, 0), ((group, DOWN_WIN * group - CHUNK), (0, 0)))
    window = lax.dynamic_slice_in_dim(window, group - phase_down, DOWN_WIN * group, 0)
    down = window.reshape(DOWN_WIN, MEMBERS, SPAN, LANES).transpose(1, 2, 0, 3)
    return pack_slots(gu, down, chunk)


def pack_slots(gu, down, chunk):
    flat = gu.reshape(MEMBERS, GU_WIN * 5, LANES), down.reshape(MEMBERS, DOWN_WIN * SPAN, LANES)
    plain = jnp.pad(flat[0], ((0, 0), (0, SLOTS - GU_WIN * 5), (0, 0))) + jnp.pad(
        flat[1], ((0, 0), (DOWN_SLOT, SLOTS - DOWN_SLOT - DOWN_WIN * SPAN), (0, 0))
    )
    mixed = jnp.concatenate(
        [
            gu[:, :, :MIX_GU].reshape(MEMBERS, 5 * MIX_GU, LANES),
            down[:, :, MIX_SKIP : MIX_SKIP + 8].reshape(MEMBERS, 8 * SPAN, LANES),
        ],
        axis=1,
    )
    mixed = jnp.pad(mixed, ((0, 0), (0, SLOTS - 5 * MIX_GU - 8 * SPAN), (0, 0)))
    return jnp.where(chunk == DOWN_FIRST, mixed, plain)


def join_chunk(cut, chunk):
    phase, phase_down, is_gu, is_down = chunk_places(chunk)
    gu = cut[:, : GU_WIN * 5].reshape(MEMBERS, 5, GU_WIN, LANES)
    mixed = cut[:, : 5 * MIX_GU].reshape(MEMBERS, 5, MIX_GU, LANES)
    mixed = jnp.pad(mixed, ((0, 0), (0, 0), (0, GU_WIN - MIX_GU), (0, 0)))
    gu = jnp.where(chunk == DOWN_FIRST, mixed, gu)
    gu = gu.transpose(1, 2, 0, 3).reshape(GU_WIN * 5, MEMBERS * LANES)
    gu = mm_nt(gu, lane_matrix())
    gu = gu.reshape(5, GU_WIN, 8, LANES).transpose(1, 0, 2, 3).reshape(GU_WIN, WIDE, LANES)
    gu = gu[:, :TILES].reshape(GU_WIN * TILES, LANES)
    gu = lax.dynamic_slice_in_dim(gu, phase, CHUNK, 0)
    down = cut[:, DOWN_SLOT : DOWN_SLOT + DOWN_WIN * SPAN].reshape(MEMBERS, SPAN, DOWN_WIN, LANES)
    mixed = cut[:, 5 * MIX_GU : 5 * MIX_GU + 8 * SPAN].reshape(MEMBERS, SPAN, 8, LANES)
    mixed = jnp.pad(mixed, ((0, 0), (0, 0), (MIX_SKIP, DOWN_WIN - MIX_SKIP - 8), (0, 0)))
    down = jnp.where(chunk == DOWN_FIRST, mixed, down).transpose(2, 0, 1, 3)
    down = down.reshape(DOWN_WIN * MEMBERS * SPAN, LANES)
    down = lax.dynamic_slice_in_dim(down, phase_down, CHUNK, 0)
    return gu, is_gu, down, is_down


def gather_mlp(cut):
    cut = lax.all_to_all(cut, ("c", "y"), 0, 0, tiled=True)
    copies = jnp.broadcast_to(cut[None], (16,) + cut.shape)
    return lax.all_to_all(copies, ("z", "xl", "xh"), 0, 0, tiled=True)


def scatter_mlp(pieces):
    pieces = lax.all_to_all(pieces, ("z", "xl", "xh"), 0, 0, tiled=True)
    part = jnp.sum(pieces.astype(F32), axis=0).astype(BF)
    return lax.all_to_all(part, ("c", "y"), 0, 0, tiled=True)


def chunk_index(chunk):
    return (chunk >> 5) * 4 + ((chunk >> 4) & 1) * 2 + (chunk & 1), (chunk >> 1) & 7


def gu_moves(chunk):
    start = (chunk * CHUNK - GU_START) // TILES
    low, high = max(0, -start), min(GU_WIN, 2 * D - start)
    step = MIX_GU if chunk == DOWN_FIRST else GU_WIN
    return [(j * step + low, start + low, high - low, j * LANES) for j in range(5)]


def down_moves(chunk):
    start = (chunk * CHUNK - DOWN_START) // (MEMBERS * SPAN)
    if chunk == DOWN_FIRST:
        return [(5 * MIX_GU + c * 8, 0, 8, c * LANES) for c in range(SPAN)]
    high = min(DOWN_WIN, UNITS - start)
    return [(DOWN_SLOT + c * DOWN_WIN, start, high, c * LANES) for c in range(SPAN)]


STAGES = 4


def assemble_kernel(pieces, gate, up, down, stage, gu_sum, down_sum):
    gu_sum[...] = jnp.zeros_like(gu_sum)
    down_sum[...] = jnp.zeros_like(down_sum)
    for chunk in range(GU_FIRST, 128):
        slot = stage.at[chunk % STAGES]
        a, b = chunk_index(chunk)
        slot[...] = pieces[a, b].astype(F32)
        if chunk <= GU_LAST:
            for at, row, count, lane in gu_moves(chunk):
                gu_sum[row : row + count, lane : lane + LANES] += slot[at : at + count, :]
        if chunk >= DOWN_FIRST:
            for at, row, count, lane in down_moves(chunk):
                down_sum[row : row + count, lane : lane + LANES] += slot[at : at + count, :]
    gate[...] = gu_sum[:D, :].astype(BF)
    up[...] = gu_sum[D:, :].astype(BF)
    down[...] = down_sum[...].astype(BF)


def dissolve_kernel(gate, up, down, pieces, stage, gu, down_wide):
    gu[:D, :] = gate[...].astype(F32)
    gu[D:, :] = up[...].astype(F32)
    down_wide[...] = down[...].astype(F32)
    stage[...] = jnp.zeros_like(stage)
    for chunk in range(128):
        a, b = chunk_index(chunk)
        if chunk < GU_FIRST:
            pieces[a, b] = jnp.zeros((SLOTS, LANES), BF)
            continue
        slot = stage.at[chunk % STAGES]
        if chunk <= GU_LAST:
            for at, row, count, lane in gu_moves(chunk):
                slot[at : at + count, :] = gu[row : row + count, lane : lane + LANES]
        if chunk >= DOWN_FIRST:
            for at, row, count, lane in down_moves(chunk):
                slot[at : at + count, :] = down_wide[row : row + count, lane : lane + LANES]
        pieces[a, b] = slot[...].astype(BF)


def vmem(count):
    return [pl.BlockSpec(memory_space=pltpu.VMEM)] * count


def params_of(megabytes):
    return pltpu.CompilerParams(vmem_limit_bytes=megabytes << 20)


def assemble(pieces):
    return pl.pallas_call(
        assemble_kernel,
        in_specs=vmem(1),
        out_specs=vmem(3),
        out_shape=[
            jax.ShapeDtypeStruct((D, UNITS), BF),
            jax.ShapeDtypeStruct((D, UNITS), BF),
            jax.ShapeDtypeStruct((UNITS, D), BF),
        ],
        scratch_shapes=[
            pltpu.VMEM((STAGES, SLOTS, LANES), F32),
            pltpu.VMEM((2 * D, UNITS), F32),
            pltpu.VMEM((UNITS, D), F32),
        ],
        compiler_params=params_of(32),
        cost_estimate=pl.CostEstimate(flops=10 << 20, bytes_accessed=20 << 20, transcendentals=0),
        name="assemble",
    )(pieces)


def dissolve(gate, up, down):
    return pl.pallas_call(
        dissolve_kernel,
        in_specs=vmem(3),
        out_specs=vmem(1)[0],
        out_shape=jax.ShapeDtypeStruct((16, 8, SLOTS, LANES), BF),
        scratch_shapes=[
            pltpu.VMEM((STAGES, SLOTS, LANES), F32),
            pltpu.VMEM((2 * D, UNITS), F32),
            pltpu.VMEM((UNITS, D), F32),
        ],
        compiler_params=params_of(32),
        cost_estimate=pl.CostEstimate(flops=10 << 20, bytes_accessed=20 << 20, transcendentals=0),
        name="dissolve",
    )(gate, up, down)


HALF = 8 * CHUNK
ROW_QB = SPAN + Q_ROWS
ROW_K = ROW_QB + SPAN
ROW_KB = ROW_K + D
ROW_V = ROW_KB + 1
ROW_VB = ROW_V + D
ROW_O = ROW_VB + 1
ROW_G2 = ROW_O + Q_ROWS
QKV = D + 2 * LANES


def unpack_kernel(core, own, other, qkv_w, qkv_b, out_w, gain_one, gain_two, rows):
    c = core[0]
    for j in range(8):
        rows[c, j * CHUNK : (j + 1) * CHUNK, :] = own[j].astype(F32)[:CHUNK]
        rows[1 - c, j * CHUNK : (j + 1) * CHUNK, :] = other[j].astype(F32)[:CHUNK]
    for t in range(SPAN):
        lanes = slice(t * LANES, (t + 1) * LANES)
        gain_one[:, lanes] = rows[0, t : t + 1, :]
        qkv_w[:, lanes] = rows[0, pl.ds(SPAN + t, D, stride=SPAN), :].astype(BF)
        qkv_b[:, lanes] = rows[0, ROW_QB + t : ROW_QB + t + 1, :]
        out_w[:, lanes] = rows[1, pl.ds(ROW_O - HALF + t, D, stride=SPAN), :].astype(BF)
        gain_two[:, lanes] = rows[1, ROW_G2 - HALF + t : ROW_G2 - HALF + t + 1, :]
    qkv_w[:, D : D + LANES] = rows[0, ROW_K : ROW_K + D, :].astype(BF)
    qkv_b[:, D : D + LANES] = rows[0, ROW_KB : ROW_KB + 1, :]
    near = HALF - ROW_V
    value = jnp.concatenate([rows[0, ROW_V:HALF, :], rows[1, : D - near, :]], axis=0)
    qkv_w[:, D + LANES :] = value.astype(BF)
    qkv_b[:, D + LANES :] = rows[1, ROW_VB - HALF : ROW_VB - HALF + 1, :]


def unpack(core, own, other):
    return pl.pallas_call(
        unpack_kernel,
        in_specs=[pl.BlockSpec(memory_space=pltpu.SMEM)] + vmem(2),
        out_specs=vmem(5),
        out_shape=[
            jax.ShapeDtypeStruct((D, QKV), BF),
            jax.ShapeDtypeStruct((1, QKV), F32),
            jax.ShapeDtypeStruct((D, D), BF),
            jax.ShapeDtypeStruct((1, D), F32),
            jax.ShapeDtypeStruct((1, D), F32),
        ],
        scratch_shapes=[pltpu.VMEM((2, HALF, LANES), F32)],
        compiler_params=params_of(32),
        cost_estimate=pl.CostEstimate(flops=10 << 20, bytes_accessed=20 << 20, transcendentals=0),
        name="unpack",
    )(core, own, other)


def pack_kernel(core, n1, dqkv, attended, grad_attn, gain_one, gain_two, out, rows):
    c = core[0]
    grad = mm_tn(n1[...], dqkv[...])
    bias = jnp.sum(dqkv[...].astype(F32), axis=0, keepdims=True)
    grad_out = mm_tn(attended[...], grad_attn[...])
    for t in range(SPAN):
        lanes = slice(t * LANES, (t + 1) * LANES)
        rows[0, t : t + 1, :] = gain_one[:, lanes]
        rows[0, pl.ds(SPAN + t, D, stride=SPAN), :] = grad[:, lanes]
        rows[0, ROW_QB + t : ROW_QB + t + 1, :] = bias[:, lanes]
        rows[1, pl.ds(ROW_O - HALF + t, D, stride=SPAN), :] = grad_out[:, lanes]
        rows[1, ROW_G2 - HALF + t : ROW_G2 - HALF + t + 1, :] = gain_two[:, lanes]
    rows[0, ROW_K : ROW_K + D, :] = grad[:, D : D + LANES]
    rows[0, ROW_KB : ROW_KB + 1, :] = bias[:, D : D + LANES]
    near = HALF - ROW_V
    rows[0, ROW_V:HALF, :] = grad[:near, D + LANES :]
    rows[1, : D - near, :] = grad[near:, D + LANES :]
    rows[1, ROW_VB - HALF : ROW_VB - HALF + 1, :] = bias[:, D + LANES :]
    rows[1, GU_START - HALF :, :] = jnp.zeros((2 * HALF - GU_START, LANES), F32)
    tail = jnp.zeros((PARTS * PART_ROWS - CHUNK, LANES), F32)
    for j in range(8):
        out[0, j] = jnp.concatenate([rows[c, j * CHUNK : (j + 1) * CHUNK, :], tail]).astype(BF)
        out[1, j] = jnp.concatenate([rows[1 - c, j * CHUNK : (j + 1) * CHUNK, :], tail]).astype(BF)


def pack(core, n1, dqkv, attended, grad_attn, gain_one, gain_two):
    return pl.pallas_call(
        pack_kernel,
        in_specs=[pl.BlockSpec(memory_space=pltpu.SMEM)] + vmem(6),
        out_specs=vmem(1)[0],
        out_shape=jax.ShapeDtypeStruct((2, 8, PARTS * PART_ROWS, LANES), BF),
        scratch_shapes=[pltpu.VMEM((2, HALF, LANES), F32)],
        compiler_params=params_of(32),
        cost_estimate=pl.CostEstimate(flops=500 << 20, bytes_accessed=20 << 20, transcendentals=0),
        name="pack",
    )(core, n1, dqkv, attended, grad_attn, gain_one, gain_two)


def mlp_kernel(x, dy, gate_w, up_w, down_w, y, dx, grad_gate, grad_up, grad_down, sum_gate, sum_up, sum_down):
    step = pl.program_id(0)

    @pl.when(step == 0)
    def _():
        sum_gate[...] = jnp.zeros_like(sum_gate)
        sum_up[...] = jnp.zeros_like(sum_up)
        sum_down[...] = jnp.zeros_like(sum_down)

    gate = mm(x[...], gate_w[...])
    up = mm(x[...], up_w[...])
    dh = mm_nt(dy[...], down_w[...])
    sigmoid = 1.0 / (1.0 + jnp.exp(-gate))
    silu = gate * sigmoid
    hidden = (silu * up).astype(BF)
    dg = (dh * up * sigmoid * (1.0 + gate * (1.0 - sigmoid))).astype(BF)
    du = (dh * silu).astype(BF)
    y[...] = mm(hidden, down_w[...]).astype(BF)
    dx[...] = (mm_nt(dg, gate_w[...]) + mm_nt(du, up_w[...])).astype(BF)
    sum_gate[...] += mm_tn(x[...], dg)
    sum_up[...] += mm_tn(x[...], du)
    sum_down[...] += mm_tn(hidden, dy[...])

    @pl.when(step == pl.num_programs(0) - 1)
    def _():
        grad_gate[...] = sum_gate[...].astype(BF)
        grad_up[...] = sum_up[...].astype(BF)
        grad_down[...] = sum_down[...].astype(BF)


def feed_forward(x, dy, gate_w, up_w, down_w):
    tokens = x.shape[0]
    block = 256
    whole = lambda r, c: pl.BlockSpec((r, c), lambda i: (0, 0))
    part = pl.BlockSpec((block, D), lambda i: (i, 0))
    return pl.pallas_call(
        mlp_kernel,
        grid=(tokens // block,),
        in_specs=[part, part, whole(D, UNITS), whole(D, UNITS), whole(UNITS, D)],
        out_specs=[part, part, whole(D, UNITS), whole(D, UNITS), whole(UNITS, D)],
        out_shape=[
            jax.ShapeDtypeStruct((tokens, D), BF),
            jax.ShapeDtypeStruct((tokens, D), BF),
            jax.ShapeDtypeStruct((D, UNITS), BF),
            jax.ShapeDtypeStruct((D, UNITS), BF),
            jax.ShapeDtypeStruct((UNITS, D), BF),
        ],
        scratch_shapes=[pltpu.VMEM((D, UNITS), F32), pltpu.VMEM((D, UNITS), F32), pltpu.VMEM((UNITS, D), F32)],
        compiler_params=params_of(48),
        cost_estimate=pl.CostEstimate(
            flops=18 * tokens * D * UNITS, bytes_accessed=16 << 20, transcendentals=tokens * UNITS
        ),
        name="feed_forward",
    )(x, dy, gate_w, up_w, down_w)


def allowed_keys(seg_q, seg_k, place_q, place_k):
    return (seg_q[...] == seg_k[...]) & (place_k[...] <= place_q[...])


def attend_kernel(q, k, v, seg_q, seg_k, place_q, place_k, out, lse):
    scores = mm_nt(q[0], k[0]) * (HEAD_DIM**-0.5)
    scores = jnp.where(allowed_keys(seg_q, seg_k, place_q, place_k), scores, -1e30)
    peak = jnp.max(scores, axis=1, keepdims=True)
    raised = jnp.exp(scores - peak)
    total = jnp.sum(raised, axis=1, keepdims=True)
    shares = (raised * (1.0 / total)).astype(BF)
    out[0] = mm(shares, v[0]).astype(BF)
    lse[0] = peak + jnp.log(total)


def attend_back_kernel(q, k, v, do, lse, seg_q, seg_k, place_q, place_k, dq, dk, dv):
    head = lax.rem(pl.program_id(0), GROUP)
    scale = HEAD_DIM**-0.5
    scores = mm_nt(q[0], k[0]) * scale
    scores = jnp.where(allowed_keys(seg_q, seg_k, place_q, place_k), scores, -1e30)
    shares = jnp.exp(scores - lse[0])
    grad_shares = mm_nt(do[0], v[0])
    delta = jnp.sum(shares * grad_shares, axis=1, keepdims=True)
    grad_scores = (shares * (grad_shares - delta)).astype(BF)
    dq[0] = mm(grad_scores, k[0]) * scale
    grad_k = mm_tn(q[0], grad_scores) * scale
    grad_v = mm_tn(do[0], shares.astype(BF))

    @pl.when(head == 0)
    def _():
        dk[0] = grad_k
        dv[0] = grad_v

    @pl.when(head != 0)
    def _():
        dk[0] += grad_k
        dv[0] += grad_v


def head_spec(rows, cols):
    return pl.BlockSpec((1, rows, cols), lambda h: (h, 0, 0))


def kv_spec(rows, cols):
    return pl.BlockSpec((1, rows, cols), lambda h: (h // GROUP, 0, 0))


def full_spec(rows, cols):
    return pl.BlockSpec((rows, cols), lambda h: (0, 0))


def mask_specs(tokens, length):
    return [full_spec(tokens, 1), full_spec(1, length), full_spec(tokens, 1), full_spec(1, length)]


def attend(q, k, v, masks):
    tokens, length = q.shape[1], k.shape[1]
    return pl.pallas_call(
        attend_kernel,
        grid=(HEADS,),
        in_specs=[head_spec(tokens, HEAD_DIM), kv_spec(length, HEAD_DIM), kv_spec(length, HEAD_DIM)]
        + mask_specs(tokens, length),
        out_specs=[head_spec(tokens, HEAD_DIM), head_spec(tokens, 1)],
        out_shape=[
            jax.ShapeDtypeStruct((HEADS, tokens, HEAD_DIM), BF),
            jax.ShapeDtypeStruct((HEADS, tokens, 1), F32),
        ],
        compiler_params=pltpu.CompilerParams(vmem_limit_bytes=32 << 20),
        cost_estimate=pl.CostEstimate(
            flops=4 * HEADS * tokens * length * HEAD_DIM,
            bytes_accessed=2 << 20,
            transcendentals=HEADS * tokens * length,
        ),
        name="attend",
    )(q, k, v, *masks)


def attend_back(q, k, v, do, lse, masks):
    tokens, length = q.shape[1], k.shape[1]
    return pl.pallas_call(
        attend_back_kernel,
        grid=(HEADS,),
        in_specs=[
            head_spec(tokens, HEAD_DIM),
            kv_spec(length, HEAD_DIM),
            kv_spec(length, HEAD_DIM),
            head_spec(tokens, HEAD_DIM),
            head_spec(tokens, 1),
        ]
        + mask_specs(tokens, length),
        out_specs=[head_spec(tokens, HEAD_DIM), kv_spec(HEAD_DIM, length), kv_spec(HEAD_DIM, length)],
        out_shape=[
            jax.ShapeDtypeStruct((HEADS, tokens, HEAD_DIM), F32),
            jax.ShapeDtypeStruct((KV_HEADS, HEAD_DIM, length), F32),
            jax.ShapeDtypeStruct((KV_HEADS, HEAD_DIM, length), F32),
        ],
        compiler_params=pltpu.CompilerParams(vmem_limit_bytes=32 << 20),
        cost_estimate=pl.CostEstimate(
            flops=10 * HEADS * tokens * length * HEAD_DIM,
            bytes_accessed=4 << 20,
            transcendentals=HEADS * tokens * length,
        ),
        name="attend_back",
    )(q, k, v, do, lse, *masks)


def rope_tables(positions):
    half_dim = HEAD_DIM // 2
    freqs = ROPE_BASE ** (-(jnp.arange(half_dim, dtype=F32) * 2.0) / HEAD_DIM)
    angles = positions.astype(F32)[:, None] * freqs
    cosine, sine = jnp.cos(angles), jnp.sin(angles)
    return jnp.concatenate([cosine, cosine], axis=1), jnp.concatenate([-sine, sine], axis=1)


def rotate(values, cosine, sine):
    heads = values.shape[1] // HEAD_DIM
    half_dim = HEAD_DIM // 2
    lane = lax.broadcasted_iota(jnp.int32, values.shape, 1) % HEAD_DIM
    other = jnp.where(
        lane < half_dim, jnp.roll(values, -half_dim, axis=1), jnp.roll(values, half_dim, axis=1)
    )
    return values * jnp.tile(cosine, (1, heads)) + other * jnp.tile(sine, (1, heads))


def norm_back(token_rows, recip, gain, grad_normed):
    scaled = grad_normed * gain
    grad_rows = recip * scaled - token_rows * recip**3 * jnp.mean(
        scaled * token_rows, axis=-1, keepdims=True
    )
    return grad_rows, jnp.sum(grad_normed * token_rows * recip, axis=0)


def to_heads(values, heads):
    return values.reshape(-1, heads, HEAD_DIM).transpose(1, 0, 2)


def from_heads(values):
    heads, tokens, _ = values.shape
    return values.transpose(1, 0, 2).reshape(tokens, heads * HEAD_DIM)


def spread(block):
    near = jnp.stack([block] + [xor(block, "y", step, 4) for step in range(1, 4)])
    return jnp.concatenate([near, swap(near, "c")])


def collect(partial):
    near = partial[:4].astype(F32) + swap(partial[4:], "c").astype(F32)
    total = near[0]
    low = near[1:].astype(BF)
    for step in range(1, 4):
        total = total + xor(low[step - 1], "y", step, 4).astype(F32)
    return total


def local(inputs, params, segments, cotangent):
    tokens = inputs.shape[1]
    length = segments.shape[1]
    x = inputs[0]
    grad_out = cotangent[0]
    chunk = lax.axis_index(("z", "xl", "c", "y", "xh"))
    place = lax.axis_index(("y", "xh"))

    core = lax.axis_index("c").astype(jnp.int32).reshape(1)
    rows = params.reshape(CHUNK, LANES).astype(BF)
    own, other = gather_attention(rows)
    qkv_w, qkv_b, out_w, gain_one, gain_two = unpack(core, own, other)
    gate_w, up_w, down_w = assemble(gather_mlp(cut_chunk(rows, chunk)))
    grad_low = grad_out.astype(BF)
    dy = spread(grad_low).reshape(-1, D)

    seg_row = segments[0]
    place_mine = place * tokens + jnp.arange(tokens, dtype=jnp.int32)
    seg_mine = lax.dynamic_slice_in_dim(seg_row, place * tokens, tokens, 0)
    place_keys = jnp.arange(length, dtype=jnp.int32)
    masks = (seg_mine[:, None], seg_row[None, :], place_mine[:, None], place_keys[None, :])
    doc_start = jnp.sum((seg_row[None, :] < seg_mine[:, None]).astype(jnp.int32), axis=1)
    cosine, sine = rope_tables(place_mine - doc_start)

    recip_one = lax.rsqrt(jnp.mean(x * x, axis=-1, keepdims=True) + EPS)
    normed_one = (x * recip_one * gain_one).astype(BF)
    qkv = mm(normed_one, qkv_w) + qkv_b
    k = rotate(qkv[:, D : D + 128], cosine, sine).astype(BF)
    kv = jnp.concatenate([k, qkv[:, D + 128 :].astype(BF)], axis=1)
    kv_all = lax.all_to_all(jnp.broadcast_to(kv[None], (8,) + kv.shape), ("y", "xh"), 0, 0, tiled=True)
    kv_all = kv_all.reshape(length, 256)
    q = rotate(qkv[:, :D], cosine, sine).astype(BF)
    q_heads = to_heads(q, HEADS)
    k_heads = to_heads(kv_all[:, :128], KV_HEADS)
    v_heads = to_heads(kv_all[:, 128:], KV_HEADS)
    out_heads, lse = attend(q_heads, k_heads, v_heads, masks)
    attended = from_heads(out_heads)
    mid = x + mm(attended, out_w)
    recip_two = lax.rsqrt(jnp.mean(mid * mid, axis=-1, keepdims=True) + EPS)
    normed_two = (mid * recip_two * gain_two).astype(BF)

    n2 = spread(normed_two).reshape(-1, D)
    mlp, grad_n2, grad_gate_w, grad_up_w, grad_down_w = feed_forward(n2, dy, gate_w, up_w, down_w)
    grad_n2 = collect(grad_n2.reshape(8, tokens, D))
    mlp_grads = scatter_mlp(dissolve(grad_gate_w, grad_up_w, grad_down_w))

    grad_mid_norm, grad_gain_two = norm_back(mid, recip_two, gain_two, grad_n2)
    grad_mid = grad_out + grad_mid_norm
    grad_attn = grad_mid.astype(BF)
    grad_attended = mm_nt(grad_attn, out_w).astype(BF)
    dq, dk, dv = attend_back(
        q_heads, k_heads, v_heads, to_heads(grad_attended, HEADS), lse, masks
    )
    outputs = mid + collect(mlp.reshape(8, tokens, D))
    dkv = jnp.concatenate([dk, dv]).reshape(4 * HEAD_DIM, length).T.astype(BF)
    dkv = lax.all_to_all(dkv.reshape(8, tokens, 4 * HEAD_DIM), ("y", "xh"), 0, 0, tiled=True)
    dkv = jnp.sum(dkv.astype(F32), axis=0)
    dqp = rotate(from_heads(dq), cosine, -sine).astype(BF)
    dkp = rotate(dkv[:, :128], cosine, -sine).astype(BF)
    dqkv = jnp.concatenate([dqp, dkp, dkv[:, 128:].astype(BF)], axis=1)
    grad_n1 = mm_nt(dqkv, qkv_w)
    grad_rows, grad_gain_one = norm_back(x, recip_one, gain_one, grad_n1)
    input_grad = grad_mid + grad_rows

    packed = pack(core, normed_one, dqkv, attended, grad_attn, grad_gain_one[None], grad_gain_two[None])
    attn_mine = scatter_attention(packed[0], packed[1]).astype(F32)

    gu_mine, is_gu, down_mine, is_down = join_chunk(mlp_grads, chunk)
    flat_row = chunk * CHUNK + jnp.arange(CHUNK, dtype=jnp.int32)[:, None]
    param_grad = jnp.where(flat_row < GU_START, attn_mine, 0.0)
    param_grad = jnp.where(is_gu, gu_mine, param_grad)
    param_grad = jnp.where(is_down, down_mine.astype(F32), param_grad)
    return outputs[None], input_grad[None], param_grad.reshape(-1)


def solution(mesh):
    fine = Mesh(mesh.devices.reshape(4, 2, 2, 4, 2), ("z", "xl", "c", "y", "xh"))
    dp, seq = ("z", "xl", "c"), ("y", "xh")
    placed = (P(dp, seq, None), P(dp + seq), P(dp, None), P(dp, seq, None))
    return jax.shard_map(
        local,
        mesh=fine,
        in_specs=placed,
        out_specs=(P(dp, seq, None), P(dp, seq, None), P(dp + seq)),
        check_vma=False,
    )
```

```python
import functools

import jax
import jax.numpy as jnp
import numpy as np
from jax import lax
from jax.experimental import pallas as pl
from jax.experimental.pallas import tpu as pltpu
from jax.sharding import Mesh, PartitionSpec as P

D = 896
FF = 4864
HEADS = 14
KV_HEADS = 2
HEAD_DIM = 64
GROUP = HEADS // KV_HEADS
EPS = 1e-06
ROPE_BASE = 1000000.0
LANES = 128

CHUNK = 911
TILES = FF // LANES
WIDE = 40
SPAN = D // LANES
Q_ROWS = D * SPAN
GU_START = SPAN + Q_ROWS + SPAN + D + 1 + D + 1 + Q_ROWS + SPAN
GU_ROWS = 2 * D * TILES
DOWN_START = GU_START + GU_ROWS
DOWN_ROWS = FF * SPAN
ATTN_CHUNKS = 16
MEMBERS = 8
UNITS = 640
GU_WIN = 25
DOWN_WIN = 18
SLOTS = 128
DOWN_SLOT = 2
PARTS = 8
PART_ROWS = 120
GU_FIRST, GU_LAST = 15, 90
DOWN_FIRST = 90
MIX_GU = 13
MIX_SKIP = 9

BF = jnp.bfloat16
F32 = jnp.float32


def dot(left, right, dims):
    return lax.dot_general(left, right, (dims, ((), ())), preferred_element_type=F32)


def mm(left, right):
    return dot(left, right, ((1,), (0,)))


def mm_nt(left, right):
    return dot(left, right, ((1,), (1,)))


def mm_tn(left, right):
    return dot(left, right, ((0,), (0,)))


def swap(value, axis):
    return lax.ppermute(value, axis, [(0, 1), (1, 0)])


def xor(value, axis, step, size):
    return lax.ppermute(value, axis, [(i, i ^ step) for i in range(size)])


def scatter_rows(rows):
    z, xl = lax.axis_index("z"), lax.axis_index("xl")
    parts = jnp.pad(rows, ((0, PARTS * PART_ROWS - CHUNK), (0, 0))).reshape(2, 4, PART_ROWS, LANES)
    part = jnp.where(xl == 0, parts[0], lax.ppermute(parts[1], "xl", [(0, 1)]))
    part = jnp.where(z == 0, part[:2], lax.ppermute(part[2:], "z", [(0, 2)]))
    return jnp.where(z % 2 == 0, part[0], lax.ppermute(part[1], "z", [(0, 1), (2, 3)]))


def gather_rows(part):
    copies = jnp.broadcast_to(part[None], (8 * PARTS, PART_ROWS, LANES))
    own = lax.all_to_all(copies, ("y", "xh", "xl", "z"), 0, 0, tiled=True)
    own = own.reshape(8, PARTS * PART_ROWS, LANES)
    return own, swap(own, "c")


def scatter_attention(own, other):
    half = (own.astype(F32) + swap(other, "c").astype(F32)).astype(BF)
    half = half.reshape(8 * PARTS, PART_ROWS, LANES)
    half = lax.all_to_all(half, ("y", "xh", "xl", "z"), 0, 0, tiled=True)
    part = jnp.sum(half.astype(F32), axis=0).astype(BF)
    copies = jnp.broadcast_to(part[None], (PARTS, PART_ROWS, LANES))
    parts = lax.all_to_all(copies, ("xl", "z"), 0, 0, tiled=True)
    return parts.reshape(-1, LANES)[:CHUNK]


def lane_order():
    m = np.arange(8)[:, None]
    lane = np.arange(LANES)[None, :]
    target = (lane % MEMBERS) * LANES + m * 16 + lane // MEMBERS
    return jnp.asarray(target.reshape(-1), jnp.int32)


def lane_matrix():
    target = lane_order()
    return (target[:, None] == jnp.arange(1024, dtype=jnp.int32)[None, :]).astype(BF)


def chunk_places(chunk):
    base = chunk * CHUNK - GU_START
    first = base // TILES
    base_down = chunk * CHUNK - DOWN_START
    first_down = base_down // (MEMBERS * SPAN)
    local = jnp.arange(CHUNK, dtype=jnp.int32)[:, None]
    is_gu = (base + local >= 0) & (base + local < GU_ROWS)
    is_down = (base_down + local >= 0) & (base_down + local < DOWN_ROWS)
    return base - first * TILES, base_down - first_down * MEMBERS * SPAN, is_gu, is_down


def cut_chunk(rows, chunk):
    phase, phase_down, is_gu, is_down = chunk_places(chunk)
    window = jnp.pad(jnp.where(is_gu, rows, 0), ((TILES, TILES + 1), (0, 0)))
    window = lax.dynamic_slice_in_dim(window, TILES - phase, GU_WIN * TILES, 0)
    window = jnp.pad(window.reshape(GU_WIN, TILES, LANES), ((0, 0), (0, WIDE - TILES), (0, 0)))
    window = window.reshape(GU_WIN, 5, 8, LANES).transpose(1, 0, 2, 3).reshape(GU_WIN * 5, 8 * LANES)
    gu = mm(window, lane_matrix()).astype(BF)
    gu = gu.reshape(5, GU_WIN, MEMBERS, LANES).transpose(2, 0, 1, 3)
    group = MEMBERS * SPAN
    window = jnp.pad(jnp.where(is_down, rows, 0), ((group, DOWN_WIN * group - CHUNK), (0, 0)))
    window = lax.dynamic_slice_in_dim(window, group - phase_down, DOWN_WIN * group, 0)
    down = window.reshape(DOWN_WIN, MEMBERS, SPAN, LANES).transpose(1, 2, 0, 3)
    return pack_slots(gu, down, chunk)


def pack_slots(gu, down, chunk):
    flat = gu.reshape(MEMBERS, GU_WIN * 5, LANES), down.reshape(MEMBERS, DOWN_WIN * SPAN, LANES)
    plain = jnp.pad(flat[0], ((0, 0), (0, SLOTS - GU_WIN * 5), (0, 0))) + jnp.pad(
        flat[1], ((0, 0), (DOWN_SLOT, SLOTS - DOWN_SLOT - DOWN_WIN * SPAN), (0, 0))
    )
    mixed = jnp.concatenate(
        [
            gu[:, :, :MIX_GU].reshape(MEMBERS, 5 * MIX_GU, LANES),
            down[:, :, MIX_SKIP : MIX_SKIP + 8].reshape(MEMBERS, 8 * SPAN, LANES),
        ],
        axis=1,
    )
    mixed = jnp.pad(mixed, ((0, 0), (0, SLOTS - 5 * MIX_GU - 8 * SPAN), (0, 0)))
    return jnp.where(chunk == DOWN_FIRST, mixed, plain)


def join_chunk(cut, chunk):
    phase, phase_down, is_gu, is_down = chunk_places(chunk)
    gu = cut[:, : GU_WIN * 5].reshape(MEMBERS, 5, GU_WIN, LANES)
    mixed = cut[:, : 5 * MIX_GU].reshape(MEMBERS, 5, MIX_GU, LANES)
    mixed = jnp.pad(mixed, ((0, 0), (0, 0), (0, GU_WIN - MIX_GU), (0, 0)))
    gu = jnp.where(chunk == DOWN_FIRST, mixed, gu)
    gu = gu.transpose(1, 2, 0, 3).reshape(GU_WIN * 5, MEMBERS * LANES)
    gu = mm_nt(gu, lane_matrix())
    gu = gu.reshape(5, GU_WIN, 8, LANES).transpose(1, 0, 2, 3).reshape(GU_WIN, WIDE, LANES)
    gu = gu[:, :TILES].reshape(GU_WIN * TILES, LANES)
    gu = lax.dynamic_slice_in_dim(gu, phase, CHUNK, 0)
    down = cut[:, DOWN_SLOT : DOWN_SLOT + DOWN_WIN * SPAN].reshape(MEMBERS, SPAN, DOWN_WIN, LANES)
    mixed = cut[:, 5 * MIX_GU : 5 * MIX_GU + 8 * SPAN].reshape(MEMBERS, SPAN, 8, LANES)
    mixed = jnp.pad(mixed, ((0, 0), (0, 0), (MIX_SKIP, DOWN_WIN - MIX_SKIP - 8), (0, 0)))
    down = jnp.where(chunk == DOWN_FIRST, mixed, down).transpose(2, 0, 1, 3)
    down = down.reshape(DOWN_WIN * MEMBERS * SPAN, LANES)
    down = lax.dynamic_slice_in_dim(down, phase_down, CHUNK, 0)
    return gu, is_gu, down, is_down


X = ("xl", "xh")


def ring_gather(block, axis):
    return jnp.stack([block] + [xor(block, axis, step, 4) for step in range(1, 4)])


def ring_sum(blocks, axis):
    total = blocks[0].astype(F32)
    for step in range(1, 4):
        total = total + xor(blocks[step], axis, step, 4).astype(F32)
    return total.astype(BF)


def gather_mlp_near(cut):
    return ring_gather(cut[:, : SLOTS // 2], "z"), ring_gather(cut[:, SLOTS // 2 :], X)


def gather_mlp_far(low, high):
    return ring_gather(low, X), ring_gather(high, "z")


def scatter_mlp(low, high):
    low, high = ring_sum(low, "z"), ring_sum(high, X)
    return jnp.concatenate([ring_sum(low, X), ring_sum(high, "z")], axis=1)


def chunk_index(chunk):
    return chunk >> 5, ((chunk >> 4) & 1) * 2 + (chunk & 1), (chunk >> 1) & 7


def gu_moves(chunk):
    start = (chunk * CHUNK - GU_START) // TILES
    low, high = max(0, -start), min(GU_WIN, 2 * D - start)
    step = MIX_GU if chunk == DOWN_FIRST else GU_WIN
    return [(j * step + low, start + low, high - low, j * LANES) for j in range(5)]


def down_moves(chunk):
    start = (chunk * CHUNK - DOWN_START) // (MEMBERS * SPAN)
    if chunk == DOWN_FIRST:
        return [(5 * MIX_GU + c * 8, 0, 8, c * LANES) for c in range(SPAN)]
    high = min(DOWN_WIN, UNITS - start)
    return [(DOWN_SLOT + c * DOWN_WIN, start, high, c * LANES) for c in range(SPAN)]


STAGES = 4


def assemble_kernel(here, low, high, gate, up, down, stage, gu_sum, down_sum):
    gu_sum[...] = jnp.zeros_like(gu_sum)
    down_sum[...] = jnp.zeros_like(down_sum)
    for chunk in range(GU_FIRST, 128):
        slot = stage.at[chunk % STAGES]
        z, x, member = chunk_index(chunk)
        z, x = here[0] ^ z, here[1] ^ x
        slot[: SLOTS // 2, :] = low[x, z, member].astype(F32)
        slot[SLOTS // 2 :, :] = high[z, x, member].astype(F32)
        if chunk <= GU_LAST:
            for at, row, count, lane in gu_moves(chunk):
                gu_sum[row : row + count, lane : lane + LANES] += slot[at : at + count, :]
        if chunk >= DOWN_FIRST:
            for at, row, count, lane in down_moves(chunk):
                down_sum[row : row + count, lane : lane + LANES] += slot[at : at + count, :]
    gate[...] = gu_sum[:D, :].astype(BF)
    up[...] = gu_sum[D:, :].astype(BF)
    down[...] = down_sum[...].astype(BF)


def dissolve(here, gu, down, low, high, stage):
    stage[...] = jnp.zeros_like(stage)
    for chunk in range(128):
        z, x, member = chunk_index(chunk)
        z, x = here[0] ^ z, here[1] ^ x
        if chunk < GU_FIRST:
            low[z, x, member] = jnp.zeros((SLOTS // 2, LANES), BF)
            high[x, z, member] = jnp.zeros((SLOTS // 2, LANES), BF)
            continue
        slot = stage.at[chunk % STAGES]
        if chunk <= GU_LAST:
            for at, row, count, lane in gu_moves(chunk):
                slot[at : at + count, :] = gu[row : row + count, lane : lane + LANES]
        if chunk >= DOWN_FIRST:
            for at, row, count, lane in down_moves(chunk):
                slot[at : at + count, :] = down[row : row + count, lane : lane + LANES]
        low[z, x, member] = slot[: SLOTS // 2, :].astype(BF)
        high[x, z, member] = slot[SLOTS // 2 :, :].astype(BF)


def vmem(count):
    return [pl.BlockSpec(memory_space=pltpu.VMEM)] * count


def params_of(megabytes):
    return pltpu.CompilerParams(vmem_limit_bytes=megabytes << 20)


def assemble(here, pieces):
    return pl.pallas_call(
        assemble_kernel,
        in_specs=[pl.BlockSpec(memory_space=pltpu.SMEM)] + vmem(2),
        out_specs=vmem(3),
        out_shape=[
            jax.ShapeDtypeStruct((D, UNITS), BF),
            jax.ShapeDtypeStruct((D, UNITS), BF),
            jax.ShapeDtypeStruct((UNITS, D), BF),
        ],
        scratch_shapes=[
            pltpu.VMEM((STAGES, SLOTS, LANES), F32),
            pltpu.VMEM((2 * D, UNITS), F32),
            pltpu.VMEM((UNITS, D), F32),
        ],
        compiler_params=params_of(24),
        cost_estimate=pl.CostEstimate(flops=10 << 20, bytes_accessed=20 << 20, transcendentals=0),
        name="assemble",
    )(here, *pieces)


HALF = 8 * CHUNK
ROW_QB = SPAN + Q_ROWS
ROW_K = ROW_QB + SPAN
ROW_KB = ROW_K + D
ROW_V = ROW_KB + 1
ROW_VB = ROW_V + D
ROW_O = ROW_VB + 1
ROW_G2 = ROW_O + Q_ROWS
QKV = D + 2 * LANES


def rotate_tile(tile, cosine, sine):
    half_dim = HEAD_DIM // 2
    lane = lax.broadcasted_iota(jnp.int32, tile.shape, 1)
    other = jnp.where(
        lane % HEAD_DIM < half_dim,
        pltpu.roll(tile, LANES - half_dim, 1),
        pltpu.roll(tile, half_dim, 1),
    )
    return tile * cosine + other * sine


def tile_at(t):
    return slice(t * LANES, (t + 1) * LANES)


def recip_rms(rows):
    return lax.rsqrt(jnp.mean(rows * rows, axis=1, keepdims=True) + EPS)


def norm_back(token_rows, recip, gain, grad_normed):
    scaled = grad_normed * gain
    grad_rows = recip * scaled - token_rows * (recip * recip * recip) * jnp.mean(
        scaled * token_rows, axis=1, keepdims=True
    )
    return grad_rows, jnp.sum(grad_normed * token_rows * recip, axis=0, keepdims=True)


def project_kernel(core, own, other, x, cosine, sine, q, kv, n1, qkv_w, out_w, gain_one, gain_two, rows, qkv_b):
    c = core[0]
    for j in range(8):
        rows[c, j * CHUNK : (j + 1) * CHUNK, :] = own[j].astype(F32)[:CHUNK]
        rows[1 - c, j * CHUNK : (j + 1) * CHUNK, :] = other[j].astype(F32)[:CHUNK]
    for t in range(SPAN):
        lanes = tile_at(t)
        gain_one[:, lanes] = rows[0, t : t + 1, :]
        qkv_w[:, lanes] = rows[0, pl.ds(SPAN + t, D, stride=SPAN), :].astype(BF)
        qkv_b[:, lanes] = rows[0, ROW_QB + t : ROW_QB + t + 1, :]
        out_w[:, lanes] = rows[1, pl.ds(ROW_O - HALF + t, D, stride=SPAN), :].astype(BF)
        gain_two[:, lanes] = rows[1, ROW_G2 - HALF + t : ROW_G2 - HALF + t + 1, :]
    qkv_w[:, tile_at(SPAN)] = rows[0, ROW_K : ROW_K + D, :].astype(BF)
    qkv_b[:, tile_at(SPAN)] = rows[0, ROW_KB : ROW_KB + 1, :]
    near = HALF - ROW_V
    value = jnp.concatenate([rows[0, ROW_V:HALF, :], rows[1, : D - near, :]], axis=0)
    qkv_w[:, tile_at(SPAN + 1)] = value.astype(BF)
    qkv_b[:, tile_at(SPAN + 1)] = rows[1, ROW_VB - HALF : ROW_VB - HALF + 1, :]
    n1[...] = (x[...] * recip_rms(x[...]) * gain_one[...]).astype(BF)
    qkv = mm(n1[...], qkv_w[...]) + qkv_b[...]
    for t in range(SPAN):
        q[:, tile_at(t)] = rotate_tile(qkv[:, tile_at(t)], cosine[...], sine[...]).astype(BF)
    kv[:, :LANES] = rotate_tile(qkv[:, tile_at(SPAN)], cosine[...], sine[...]).astype(BF)
    kv[:, LANES:] = qkv[:, tile_at(SPAN + 1)].astype(BF)


def project(core, own, other, x, cosine, sine):
    tokens = x.shape[0]
    return pl.pallas_call(
        project_kernel,
        in_specs=[pl.BlockSpec(memory_space=pltpu.SMEM)] + vmem(5),
        out_specs=vmem(7),
        out_shape=[
            jax.ShapeDtypeStruct((tokens, D), BF),
            jax.ShapeDtypeStruct((tokens, 2 * LANES), BF),
            jax.ShapeDtypeStruct((tokens, D), BF),
            jax.ShapeDtypeStruct((D, QKV), BF),
            jax.ShapeDtypeStruct((D, D), BF),
            jax.ShapeDtypeStruct((1, D), F32),
            jax.ShapeDtypeStruct((1, D), F32),
        ],
        scratch_shapes=[pltpu.VMEM((2, HALF, LANES), F32), pltpu.VMEM((1, QKV), F32)],
        compiler_params=params_of(24),
        cost_estimate=pl.CostEstimate(flops=300 << 20, bytes_accessed=20 << 20, transcendentals=0),
        name="project",
    )(core, own, other, x, cosine, sine)


def pack_kernel(
    core, dqp, n1, x, qkv_w, gain_one, attended, grad_attn, grad_mid, gain_two, cosine, sine, dkv,
    input_grad, mine, theirs, rows, dqkv,
):
    c = core[0]
    total = dkv[0].astype(F32)
    for j in range(1, 8):
        total = total + dkv[j].astype(F32)
    dqkv[:, :D] = dqp[...]
    dqkv[:, tile_at(SPAN)] = rotate_tile(total[:, :LANES], cosine[...], -sine[...]).astype(BF)
    dqkv[:, tile_at(SPAN + 1)] = total[:, LANES:].astype(BF)
    grad_n1 = mm_nt(dqkv[...], qkv_w[...])
    recip = recip_rms(x[...])
    grad_rows, grad_gain = norm_back(x[...], recip, gain_one[...], grad_n1)
    input_grad[...] = grad_mid[...] + grad_rows
    grad = mm_tn(n1[...], dqkv[...])
    bias = jnp.sum(dqkv[...].astype(F32), axis=0, keepdims=True)
    grad_out = mm_tn(attended[...], grad_attn[...])
    for t in range(SPAN):
        lanes = tile_at(t)
        rows[0, t : t + 1, :] = grad_gain[:, lanes]
        rows[0, pl.ds(SPAN + t, D, stride=SPAN), :] = grad[:, lanes]
        rows[0, ROW_QB + t : ROW_QB + t + 1, :] = bias[:, lanes]
        rows[1, pl.ds(ROW_O - HALF + t, D, stride=SPAN), :] = grad_out[:, lanes]
        rows[1, ROW_G2 - HALF + t : ROW_G2 - HALF + t + 1, :] = gain_two[:, lanes]
    rows[0, ROW_K : ROW_K + D, :] = grad[:, tile_at(SPAN)]
    rows[0, ROW_KB : ROW_KB + 1, :] = bias[:, tile_at(SPAN)]
    near = HALF - ROW_V
    rows[0, ROW_V:HALF, :] = grad[:near, tile_at(SPAN + 1)]
    rows[1, : D - near, :] = grad[near:, tile_at(SPAN + 1)]
    rows[1, ROW_VB - HALF : ROW_VB - HALF + 1, :] = bias[:, tile_at(SPAN + 1)]
    rows[1, GU_START - HALF :, :] = jnp.zeros((2 * HALF - GU_START, LANES), F32)
    tail = jnp.zeros((PARTS * PART_ROWS - CHUNK, LANES), F32)
    for j in range(8):
        mine[j] = jnp.concatenate([rows[c, j * CHUNK : (j + 1) * CHUNK, :], tail]).astype(BF)
        theirs[j] = jnp.concatenate([rows[1 - c, j * CHUNK : (j + 1) * CHUNK, :], tail]).astype(BF)


def pack(core, *arrays):
    tokens = arrays[1].shape[0]
    return pl.pallas_call(
        pack_kernel,
        in_specs=[pl.BlockSpec(memory_space=pltpu.SMEM)] + vmem(len(arrays)),
        out_specs=vmem(3),
        out_shape=[
            jax.ShapeDtypeStruct((tokens, D), F32),
            jax.ShapeDtypeStruct((8, PARTS * PART_ROWS, LANES), BF),
            jax.ShapeDtypeStruct((8, PARTS * PART_ROWS, LANES), BF),
        ],
        scratch_shapes=[pltpu.VMEM((2, HALF, LANES), F32), pltpu.VMEM((tokens, QKV), BF)],
        compiler_params=params_of(24),
        cost_estimate=pl.CostEstimate(flops=800 << 20, bytes_accessed=20 << 20, transcendentals=0),
        name="pack",
    )(core, *arrays)


def place_heads(blocks, k_at, v_at):
    kv = blocks[...].reshape(-1, 2 * LANES)
    for source, target in ((kv[:, :LANES], k_at), (kv[:, LANES:], v_at)):
        wide = source.astype(F32)
        low = lax.broadcasted_iota(jnp.int32, wide.shape, 1) < HEAD_DIM
        first, second = jnp.where(low, wide, 0.0), jnp.where(low, 0.0, wide)
        target[0] = first.astype(BF)
        target[1] = pltpu.roll(first, HEAD_DIM, 1).astype(BF)
        target[2] = pltpu.roll(second, HEAD_DIM, 1).astype(BF)
        target[3] = second.astype(BF)


def mark_keys(seg_q, seg_k, place_q, place_k, keep):
    allowed = (seg_q[...] == seg_k[...]) & (place_k[...] <= place_q[...])
    keep[...] = jnp.where(allowed, 1.0, 0.0)


def attend_kernel(
    q, kv, seg_q, seg_k, place_q, place_k, x, out_w, gain_two, attended, lse, mid, n2, k_at, v_at, keep
):
    place_heads(kv, k_at, v_at)
    mark_keys(seg_q, seg_k, place_q, place_k, keep)
    for t in range(SPAN):
        total_out = None
        for half in range(2):
            head = 2 * t + half
            at = (head // GROUP) * 2 + half
            scores = mm_nt(q[:, tile_at(t)], k_at[at]) * (HEAD_DIM**-0.5)
            scores = jnp.where(keep[...] > 0.0, scores, -1e30)
            peak = jnp.max(scores, axis=1, keepdims=True)
            raised = jnp.exp(scores - peak)
            total = jnp.sum(raised, axis=1, keepdims=True)
            shares = (raised * (1.0 / total)).astype(BF)
            part = mm(shares, v_at[at])
            total_out = part if total_out is None else total_out + part
            lse[:, head : head + 1] = peak + jnp.log(total)
        attended[:, tile_at(t)] = total_out.astype(BF)
    mid[...] = x[...] + mm(attended[...], out_w[...])
    n2[...] = (mid[...] * recip_rms(mid[...]) * gain_two[...]).astype(BF)


def attend_back_kernel(
    g0, g1, g2, g3, mid, gain_two, grad_out, out_w, q, kv, lse, seg_q, seg_k, place_q, place_k, cosine, sine,
    grad_mid, grad_attn, dqp, grad_gain, dkv, k_at, v_at, keep, sums,
):
    grad_n2 = g0[...] + g1[...].astype(F32) + g2[...].astype(F32) + g3[...].astype(F32)
    recip = recip_rms(mid[...])
    grad_rows, gain = norm_back(mid[...], recip, gain_two[...], grad_n2)
    grad_gain[...] = gain
    grad_mid[...] = grad_out[...] + grad_rows
    grad_attn[...] = grad_mid[...].astype(BF)
    do = mm_nt(grad_attn[...], out_w[...]).astype(BF)
    place_heads(kv, k_at, v_at)
    mark_keys(seg_q, seg_k, place_q, place_k, keep)
    sums[...] = jnp.zeros_like(sums)
    scale = HEAD_DIM**-0.5
    for t in range(SPAN):
        q_tile, do_tile = q[:, tile_at(t)], do[:, tile_at(t)]
        grad_q = None
        for half in range(2):
            head = 2 * t + half
            group = head // GROUP
            at = group * 2 + half
            scores = mm_nt(q_tile, k_at[at]) * scale
            scores = jnp.where(keep[...] > 0.0, scores, -1e30)
            shares = jnp.exp(scores - lse[:, head : head + 1])
            grad_shares = mm_nt(do_tile, v_at[at])
            delta = jnp.sum(shares * grad_shares, axis=1, keepdims=True)
            grad_scores = (shares * (grad_shares - delta)).astype(BF)
            part = mm(grad_scores, k_at[at])
            grad_q = part if grad_q is None else grad_q + part
            mine = slice(half * HEAD_DIM, (half + 1) * HEAD_DIM)
            sums[group * HEAD_DIM : (group + 1) * HEAD_DIM, :] += mm_tn(q_tile, grad_scores)[mine]
            sums[LANES + group * HEAD_DIM : LANES + (group + 1) * HEAD_DIM, :] += mm_tn(
                do_tile, shares.astype(BF)
            )[mine]
        dqp[:, tile_at(t)] = rotate_tile(grad_q * scale, cosine[...], -sine[...]).astype(BF)
    for j in range(8):
        dkv[j, :, :LANES] = (jnp.transpose(sums[:LANES, tile_at(j)]) * scale).astype(BF)
        dkv[j, :, LANES:] = jnp.transpose(sums[LANES:, tile_at(j)]).astype(BF)


def head_scratch(tokens, length):
    return [
        pltpu.VMEM((4, length, LANES), BF),
        pltpu.VMEM((4, length, LANES), BF),
        pltpu.VMEM((tokens, length), F32),
    ]


def attend(q, kv, masks, x, out_w, gain_two):
    tokens, length = q.shape[0], masks[1].shape[1]
    return pl.pallas_call(
        attend_kernel,
        in_specs=vmem(9),
        out_specs=vmem(4),
        out_shape=[
            jax.ShapeDtypeStruct((tokens, D), BF),
            jax.ShapeDtypeStruct((tokens, 16), F32),
            jax.ShapeDtypeStruct((tokens, D), F32),
            jax.ShapeDtypeStruct((tokens, D), BF),
        ],
        scratch_shapes=head_scratch(tokens, length),
        compiler_params=params_of(24),
        cost_estimate=pl.CostEstimate(
            flops=8 * HEADS * tokens * length * HEAD_DIM,
            bytes_accessed=4 << 20,
            transcendentals=HEADS * tokens * length,
        ),
        name="attend",
    )(q, kv, *masks, x, out_w, gain_two)


def attend_back(grads, mid, gain_two, grad_out, out_w, q, kv, lse, masks, cosine, sine):
    tokens, length = q.shape[0], masks[1].shape[1]
    return pl.pallas_call(
        attend_back_kernel,
        in_specs=vmem(17),
        out_specs=vmem(5),
        out_shape=[
            jax.ShapeDtypeStruct((tokens, D), F32),
            jax.ShapeDtypeStruct((tokens, D), BF),
            jax.ShapeDtypeStruct((tokens, D), BF),
            jax.ShapeDtypeStruct((1, D), F32),
            jax.ShapeDtypeStruct((8, tokens, 2 * LANES), BF),
        ],
        scratch_shapes=head_scratch(tokens, length) + [pltpu.VMEM((2 * LANES, length), F32)],
        compiler_params=params_of(24),
        cost_estimate=pl.CostEstimate(
            flops=20 * HEADS * tokens * length * HEAD_DIM,
            bytes_accessed=8 << 20,
            transcendentals=HEADS * tokens * length,
        ),
        name="attend_back",
    )(*grads, mid, gain_two, grad_out, out_w, q, kv, lse, *masks, cosine, sine)


def mlp_kernel(
    here, x_near, x_far, dy_near, dy_far, gate_w, up_w, down_w,
    y_near, y_far, dx_near, dx_far, low, high, sum_gu, sum_down, stage,
):
    halves = (x_near, dy_near, y_near, dx_near), (x_far, dy_far, y_far, dx_far)
    for first, (x_ref, dy_ref, y_ref, dx_ref) in zip((True, False), halves):
        x, dy = x_ref[...], dy_ref[...]
        gate = mm(x, gate_w[...])
        up = mm(x, up_w[...])
        dh = mm_nt(dy, down_w[...])
        sigmoid = 1.0 / (1.0 + jnp.exp(-gate))
        silu = gate * sigmoid
        hidden = (silu * up).astype(BF)
        dg = (dh * up * sigmoid * (1.0 + gate * (1.0 - sigmoid))).astype(BF)
        du = (dh * silu).astype(BF)
        y_ref[...] = mm(hidden, down_w[...]).astype(BF)
        dx_ref[...] = (mm_nt(dg, gate_w[...]) + mm_nt(du, up_w[...])).astype(BF)
        if first:
            sum_gu[:D, :] = mm_tn(x, dg)
            sum_gu[D:, :] = mm_tn(x, du)
            sum_down[...] = mm_tn(hidden, dy)
        else:
            sum_gu[:D, :] += mm_tn(x, dg)
            sum_gu[D:, :] += mm_tn(x, du)
            sum_down[...] += mm_tn(hidden, dy)
    dissolve(here, sum_gu, sum_down, low, high, stage)


def feed_forward(here, x, dy, gate_w, up_w, down_w):
    tokens = x[0].shape[0]
    sides = jax.ShapeDtypeStruct((tokens, D), BF)
    return pl.pallas_call(
        mlp_kernel,
        in_specs=[pl.BlockSpec(memory_space=pltpu.SMEM)] + vmem(7),
        out_specs=vmem(6),
        out_shape=[
            sides,
            sides,
            sides,
            sides,
            jax.ShapeDtypeStruct((4, 4, MEMBERS, SLOTS // 2, LANES), BF),
            jax.ShapeDtypeStruct((4, 4, MEMBERS, SLOTS // 2, LANES), BF),
        ],
        scratch_shapes=[
            pltpu.VMEM((2 * D, UNITS), F32),
            pltpu.VMEM((UNITS, D), F32),
            pltpu.VMEM((STAGES, SLOTS, LANES), F32),
        ],
        compiler_params=params_of(30),
        cost_estimate=pl.CostEstimate(
            flops=36 * tokens * D * UNITS, bytes_accessed=16 << 20, transcendentals=2 * tokens * UNITS
        ),
        name="feed_forward",
    )(here, *x, *dy, gate_w, up_w, down_w)


def rope_tables(positions):
    half_dim = HEAD_DIM // 2
    freqs = ROPE_BASE ** (-(jnp.arange(half_dim, dtype=F32) * 2.0) / HEAD_DIM)
    angles = positions.astype(F32)[:, None] * freqs
    cosine, sine = jnp.cos(angles), jnp.sin(angles)
    return jnp.concatenate([cosine] * 4, axis=1), jnp.concatenate([-sine, sine] * 2, axis=1)


def spread_near(block):
    return jnp.concatenate([block] + [xor(block, "y", step, 4) for step in range(1, 4)])


def spread(block):
    near = spread_near(block)
    return near, swap(near, "c")


def collect_far(near, far):
    return (near.astype(F32) + swap(far, "c").astype(F32)).reshape(4, -1, D)


def collect_near(total):
    return [total[0]] + [xor(total[step].astype(BF), "y", step, 4) for step in range(1, 4)]


def local(inputs, params, segments, cotangent):
    tokens = inputs.shape[1]
    length = segments.shape[1]
    x = inputs[0]
    grad_out = cotangent[0]
    chunk = lax.axis_index(("z", "xl", "c", "y", "xh"))
    place = lax.axis_index(("y", "xh"))
    core = lax.axis_index("c").astype(jnp.int32).reshape(1)
    here = jnp.stack([lax.axis_index("z"), lax.axis_index(X)]).astype(jnp.int32)

    seg_row = segments[0]
    place_mine = place * tokens + jnp.arange(tokens, dtype=jnp.int32)
    seg_mine = lax.dynamic_slice_in_dim(seg_row, place * tokens, tokens, 0)
    place_keys = jnp.arange(length, dtype=jnp.int32)
    masks = (seg_mine[:, None], seg_row[None, :], place_mine[:, None], place_keys[None, :])
    doc_start = jnp.sum((seg_row[None, :] < seg_mine[:, None]).astype(jnp.int32), axis=1)
    cosine, sine = rope_tables(place_mine - doc_start)

    rows = params.reshape(CHUNK, LANES).astype(BF)
    part = scatter_rows(rows)
    cut = lax.all_to_all(cut_chunk(rows, chunk), ("c", "y"), 0, 0, tiled=True)
    dy = spread(grad_out.astype(BF))
    part, cut, dy, cosine, sine = lax.optimization_barrier((part, cut, dy, cosine, sine))
    pieces = gather_mlp_near(cut)
    own, other = gather_rows(part)
    own, other, pieces = lax.optimization_barrier((own, other, pieces))
    low, high = gather_mlp_far(*pieces)

    q, kv, normed_one, qkv_w, out_w, gain_one, gain_two = project(core, own, other, x, cosine, sine)
    kv = lax.all_to_all(jnp.broadcast_to(kv[None], (8,) + kv.shape), ("y", "xh"), 0, 0, tiled=True)
    kv, high = lax.optimization_barrier((kv, high))
    attended, lse, mid, normed_two = attend(q, kv, masks, x, out_w, gain_two)
    near, low = lax.optimization_barrier((spread_near(normed_two), low))
    n2 = near, swap(near, "c")
    gate_w, up_w, down_w = assemble(here, (low, high))
    y_near, y_far, dx_near, dx_far, low, high = feed_forward(here, n2, dy, gate_w, up_w, down_w)
    grads, low, high = lax.optimization_barrier((collect_far(dx_near, dx_far), low, high))
    grads = collect_near(grads)
    part = scatter_mlp(low, high)
    grad_mid, grad_attn, dqp, grad_gain_two, dkv = attend_back(
        grads, mid, gain_two, grad_out, out_w, q, kv, lse, masks, cosine, sine
    )
    dkv, y_near, y_far = lax.optimization_barrier((dkv, y_near, y_far))
    dkv = lax.all_to_all(dkv, ("y", "xh"), 0, 0, tiled=True)
    dkv, part = lax.optimization_barrier((dkv, part))
    input_grad, mine, theirs = pack(
        core, dqp, normed_one, x, qkv_w, gain_one, attended, grad_attn, grad_mid, grad_gain_two, cosine, sine, dkv
    )
    mlp_grads = lax.all_to_all(part, ("c", "y"), 0, 0, tiled=True)
    attn_mine = scatter_attention(mine, theirs).astype(F32)
    terms = collect_near(collect_far(y_near, y_far))
    outputs = mid + terms[0] + terms[1].astype(F32) + terms[2].astype(F32) + terms[3].astype(F32)

    gu_mine, is_gu, down_mine, is_down = join_chunk(mlp_grads, chunk)
    flat_row = chunk * CHUNK + jnp.arange(CHUNK, dtype=jnp.int32)[:, None]
    param_grad = jnp.where(flat_row < GU_START, attn_mine, 0.0)
    param_grad = jnp.where(is_gu, gu_mine, param_grad)
    param_grad = jnp.where(is_down, down_mine.astype(F32), param_grad)
    return outputs[None], input_grad[None], param_grad.reshape(-1)


def solution(mesh):
    fine = Mesh(mesh.devices.reshape(4, 2, 2, 4, 2), ("z", "xl", "c", "y", "xh"))
    dp, seq = ("z", "xl", "c"), ("y", "xh")
    placed = (P(dp, seq, None), P(dp + seq), P(dp, None), P(dp, seq, None))
    return jax.shard_map(
        local,
        mesh=fine,
        in_specs=placed,
        out_specs=(P(dp, seq, None), P(dp, seq, None), P(dp + seq)),
        check_vma=False,
    )
```

```python
import functools

import jax
import jax.numpy as jnp
import numpy as np
from jax import lax
from jax.experimental import pallas as pl
from jax.experimental.pallas import tpu as pltpu
from jax.sharding import Mesh, PartitionSpec as P

D = 896
FF = 4864
HEADS = 14
KV_HEADS = 2
HEAD_DIM = 64
GROUP = HEADS // KV_HEADS
EPS = 1e-06
ROPE_BASE = 1000000.0
LANES = 128

CHUNK = 911
TILES = FF // LANES
WIDE = 40
SPAN = D // LANES
Q_ROWS = D * SPAN
GU_START = SPAN + Q_ROWS + SPAN + D + 1 + D + 1 + Q_ROWS + SPAN
GU_ROWS = 2 * D * TILES
DOWN_START = GU_START + GU_ROWS
DOWN_ROWS = FF * SPAN
ATTN_CHUNKS = 16
MEMBERS = 8
UNITS = 640
GU_WIN = 25
DOWN_WIN = 18
SLOTS = 128
DOWN_SLOT = 2
PARTS = 8
PART_ROWS = 120
GU_FIRST, GU_LAST = 15, 90
DOWN_FIRST = 90
MIX_GU = 13
MIX_SKIP = 9

BF = jnp.bfloat16
F32 = jnp.float32


def dot(left, right, dims):
    return lax.dot_general(left, right, (dims, ((), ())), preferred_element_type=F32)


def mm(left, right):
    return dot(left, right, ((1,), (0,)))


def mm_nt(left, right):
    return dot(left, right, ((1,), (1,)))


def mm_tn(left, right):
    return dot(left, right, ((0,), (0,)))


def swap(value, axis):
    return lax.ppermute(value, axis, [(0, 1), (1, 0)])


def xor(value, axis, step, size):
    return lax.ppermute(value, axis, [(i, i ^ step) for i in range(size)])


def scatter_rows(rows):
    z, xl = lax.axis_index("z"), lax.axis_index("xl")
    parts = jnp.pad(rows, ((0, PARTS * PART_ROWS - CHUNK), (0, 0))).reshape(2, 4, PART_ROWS, LANES)
    part = jnp.where(xl == 0, parts[0], lax.ppermute(parts[1], "xl", [(0, 1)]))
    part = jnp.where(z == 0, part[:2], lax.ppermute(part[2:], "z", [(0, 2)]))
    return jnp.where(z % 2 == 0, part[0], lax.ppermute(part[1], "z", [(0, 1), (2, 3)]))


def gather_rows(part):
    copies = jnp.broadcast_to(part[None], (8 * PARTS, PART_ROWS, LANES))
    own = lax.all_to_all(copies, ("y", "xh", "xl", "z"), 0, 0, tiled=True)
    return own.reshape(8, PARTS * PART_ROWS, LANES)


def scatter_rows_sum(own, other):
    half = (own.astype(F32) + swap(other, "c").astype(F32)).astype(BF)
    half = half.reshape(8 * PARTS, PART_ROWS, LANES)
    half = lax.all_to_all(half, ("y", "xh", "xl", "z"), 0, 0, tiled=True)
    return jnp.sum(half.astype(F32), axis=0)


def gather_rows_sum(part):
    copies = jnp.broadcast_to(part.astype(BF)[None], (PARTS, PART_ROWS, LANES))
    parts = lax.all_to_all(copies, ("xl", "z"), 0, 0, tiled=True)
    return parts.reshape(-1, LANES)[:CHUNK].astype(F32)


def lane_order():
    m = np.arange(8)[:, None]
    lane = np.arange(LANES)[None, :]
    target = (lane % MEMBERS) * LANES + m * 16 + lane // MEMBERS
    return jnp.asarray(target.reshape(-1), jnp.int32)


def lane_matrix():
    target = lane_order()
    return (target[:, None] == jnp.arange(1024, dtype=jnp.int32)[None, :]).astype(BF)


def chunk_places(chunk):
    base = chunk * CHUNK - GU_START
    first = base // TILES
    base_down = chunk * CHUNK - DOWN_START
    first_down = base_down // (MEMBERS * SPAN)
    local = jnp.arange(CHUNK, dtype=jnp.int32)[:, None]
    is_gu = (base + local >= 0) & (base + local < GU_ROWS)
    is_down = (base_down + local >= 0) & (base_down + local < DOWN_ROWS)
    return base - first * TILES, base_down - first_down * MEMBERS * SPAN, is_gu, is_down


def cut_chunk(rows, chunk):
    phase, phase_down, is_gu, is_down = chunk_places(chunk)
    window = jnp.pad(jnp.where(is_gu, rows, 0), ((TILES, TILES + 1), (0, 0)))
    window = lax.dynamic_slice_in_dim(window, TILES - phase, GU_WIN * TILES, 0)
    window = jnp.pad(window.reshape(GU_WIN, TILES, LANES), ((0, 0), (0, WIDE - TILES), (0, 0)))
    window = window.reshape(GU_WIN, 5, 8, LANES).transpose(1, 0, 2, 3).reshape(GU_WIN * 5, 8 * LANES)
    gu = mm(window, lane_matrix()).astype(BF)
    gu = gu.reshape(5, GU_WIN, MEMBERS, LANES).transpose(2, 0, 1, 3)
    group = MEMBERS * SPAN
    window = jnp.pad(jnp.where(is_down, rows, 0), ((group, DOWN_WIN * group - CHUNK), (0, 0)))
    window = lax.dynamic_slice_in_dim(window, group - phase_down, DOWN_WIN * group, 0)
    down = window.reshape(DOWN_WIN, MEMBERS, SPAN, LANES).transpose(1, 2, 0, 3)
    return pack_slots(gu, down, chunk)


def pack_slots(gu, down, chunk):
    flat = gu.reshape(MEMBERS, GU_WIN * 5, LANES), down.reshape(MEMBERS, DOWN_WIN * SPAN, LANES)
    plain = jnp.pad(flat[0], ((0, 0), (0, SLOTS - GU_WIN * 5), (0, 0))) + jnp.pad(
        flat[1], ((0, 0), (DOWN_SLOT, SLOTS - DOWN_SLOT - DOWN_WIN * SPAN), (0, 0))
    )
    mixed = jnp.concatenate(
        [
            gu[:, :, :MIX_GU].reshape(MEMBERS, 5 * MIX_GU, LANES),
            down[:, :, MIX_SKIP : MIX_SKIP + 8].reshape(MEMBERS, 8 * SPAN, LANES),
        ],
        axis=1,
    )
    mixed = jnp.pad(mixed, ((0, 0), (0, SLOTS - 5 * MIX_GU - 8 * SPAN), (0, 0)))
    return jnp.where(chunk == DOWN_FIRST, mixed, plain)


def join_chunk(cut, chunk):
    phase, phase_down, is_gu, is_down = chunk_places(chunk)
    gu = cut[:, : GU_WIN * 5].reshape(MEMBERS, 5, GU_WIN, LANES)
    mixed = cut[:, : 5 * MIX_GU].reshape(MEMBERS, 5, MIX_GU, LANES)
    mixed = jnp.pad(mixed, ((0, 0), (0, 0), (0, GU_WIN - MIX_GU), (0, 0)))
    gu = jnp.where(chunk == DOWN_FIRST, mixed, gu)
    gu = gu.transpose(1, 2, 0, 3).reshape(GU_WIN * 5, MEMBERS * LANES)
    gu = mm_nt(gu, lane_matrix())
    gu = gu.reshape(5, GU_WIN, 8, LANES).transpose(1, 0, 2, 3).reshape(GU_WIN, WIDE, LANES)
    gu = gu[:, :TILES].reshape(GU_WIN * TILES, LANES)
    gu = lax.dynamic_slice_in_dim(gu, phase, CHUNK, 0)
    down = cut[:, DOWN_SLOT : DOWN_SLOT + DOWN_WIN * SPAN].reshape(MEMBERS, SPAN, DOWN_WIN, LANES)
    mixed = cut[:, 5 * MIX_GU : 5 * MIX_GU + 8 * SPAN].reshape(MEMBERS, SPAN, 8, LANES)
    mixed = jnp.pad(mixed, ((0, 0), (0, 0), (MIX_SKIP, DOWN_WIN - MIX_SKIP - 8), (0, 0)))
    down = jnp.where(chunk == DOWN_FIRST, mixed, down).transpose(2, 0, 1, 3)
    down = down.reshape(DOWN_WIN * MEMBERS * SPAN, LANES)
    down = lax.dynamic_slice_in_dim(down, phase_down, CHUNK, 0)
    return gu, is_gu, down, is_down


X = ("xl", "xh")


def ring_gather(block, axis):
    return jnp.stack([block] + [xor(block, axis, step, 4) for step in range(1, 4)])


def ring_sum(blocks, axis):
    total = blocks[0].astype(F32)
    for step in range(1, 4):
        total = total + xor(blocks[step], axis, step, 4).astype(F32)
    return total.astype(BF)


def gather_mlp_near(cut):
    return ring_gather(cut[:, : SLOTS // 2], "z"), ring_gather(cut[:, SLOTS // 2 :], X)


def gather_mlp_far(low, high):
    return ring_gather(low, X), ring_gather(high, "z")


def scatter_mlp_far(low, high):
    low = lax.all_to_all(low, "z", 0, 0, tiled=True)
    return jnp.sum(low.astype(F32), axis=0).astype(BF), ring_sum(high, X)


def scatter_mlp_near(low, high):
    return jnp.concatenate([ring_sum(low, X), ring_sum(high, "z")], axis=1)


def chunk_index(chunk):
    return chunk >> 5, ((chunk >> 4) & 1) * 2 + (chunk & 1), (chunk >> 1) & 7


def gu_moves(chunk):
    start = (chunk * CHUNK - GU_START) // TILES
    low, high = max(0, -start), min(GU_WIN, 2 * D - start)
    step = MIX_GU if chunk == DOWN_FIRST else GU_WIN
    return [(j * step + low, start + low, high - low, j * LANES) for j in range(5)]


def down_moves(chunk):
    start = (chunk * CHUNK - DOWN_START) // (MEMBERS * SPAN)
    if chunk == DOWN_FIRST:
        return [(5 * MIX_GU + c * 8, 0, 8, c * LANES) for c in range(SPAN)]
    high = min(DOWN_WIN, UNITS - start)
    return [(DOWN_SLOT + c * DOWN_WIN, start, high, c * LANES) for c in range(SPAN)]


STAGES = 4


def assemble_kernel(here, low, high, gate, up, down, stage, gu_sum, down_sum):
    gu_sum[...] = jnp.zeros_like(gu_sum)
    down_sum[...] = jnp.zeros_like(down_sum)
    for chunk in range(GU_FIRST, 128):
        slot = stage.at[chunk % STAGES]
        z, x, member = chunk_index(chunk)
        z, x = here[0] ^ z, here[1] ^ x
        slot[: SLOTS // 2, :] = low[x, z, member].astype(F32)
        slot[SLOTS // 2 :, :] = high[z, x, member].astype(F32)
        if chunk <= GU_LAST:
            for at, row, count, lane in gu_moves(chunk):
                gu_sum[row : row + count, lane : lane + LANES] += slot[at : at + count, :]
        if chunk >= DOWN_FIRST:
            for at, row, count, lane in down_moves(chunk):
                down_sum[row : row + count, lane : lane + LANES] += slot[at : at + count, :]
    gate[...] = gu_sum[:D, :].astype(BF)
    up[...] = gu_sum[D:, :].astype(BF)
    down[...] = down_sum[...].astype(BF)


def dissolve(here, gu, down, low, high, stage):
    stage[...] = jnp.zeros_like(stage)
    for chunk in range(128):
        chunk_z, x, member = chunk_index(chunk)
        z, x = here[0] ^ chunk_z, here[1] ^ x
        if chunk < GU_FIRST:
            low[chunk_z, x, member] = jnp.zeros((SLOTS // 2, LANES), BF)
            high[x, z, member] = jnp.zeros((SLOTS // 2, LANES), BF)
            continue
        slot = stage.at[chunk % STAGES]
        if chunk <= GU_LAST:
            for at, row, count, lane in gu_moves(chunk):
                slot[at : at + count, :] = gu[row : row + count, lane : lane + LANES]
        if chunk >= DOWN_FIRST:
            for at, row, count, lane in down_moves(chunk):
                slot[at : at + count, :] = down[row : row + count, lane : lane + LANES]
        low[chunk_z, x, member] = slot[: SLOTS // 2, :].astype(BF)
        high[x, z, member] = slot[SLOTS // 2 :, :].astype(BF)


def vmem(count):
    return [pl.BlockSpec(memory_space=pltpu.VMEM)] * count


def params_of(megabytes):
    return pltpu.CompilerParams(vmem_limit_bytes=megabytes << 20)


def assemble(here, pieces):
    return pl.pallas_call(
        assemble_kernel,
        in_specs=[pl.BlockSpec(memory_space=pltpu.SMEM)] + vmem(2),
        out_specs=vmem(3),
        out_shape=[
            jax.ShapeDtypeStruct((D, UNITS), BF),
            jax.ShapeDtypeStruct((D, UNITS), BF),
            jax.ShapeDtypeStruct((UNITS, D), BF),
        ],
        scratch_shapes=[
            pltpu.VMEM((STAGES, SLOTS, LANES), F32),
            pltpu.VMEM((2 * D, UNITS), F32),
            pltpu.VMEM((UNITS, D), F32),
        ],
        compiler_params=params_of(24),
        cost_estimate=pl.CostEstimate(flops=10 << 20, bytes_accessed=20 << 20, transcendentals=0),
        name="assemble",
    )(here, *pieces)


HALF = 8 * CHUNK
ROW_QB = SPAN + Q_ROWS
ROW_K = ROW_QB + SPAN
ROW_KB = ROW_K + D
ROW_V = ROW_KB + 1
ROW_VB = ROW_V + D
ROW_O = ROW_VB + 1
ROW_G2 = ROW_O + Q_ROWS
QKV = D + 2 * LANES


def rotate_tile(tile, cosine, sine):
    half_dim = HEAD_DIM // 2
    lane = lax.broadcasted_iota(jnp.int32, tile.shape, 1)
    other = jnp.where(
        lane % HEAD_DIM < half_dim,
        pltpu.roll(tile, LANES - half_dim, 1),
        pltpu.roll(tile, half_dim, 1),
    )
    return tile * cosine + other * sine


def tile_at(t):
    return slice(t * LANES, (t + 1) * LANES)


def recip_rms(rows):
    return lax.rsqrt(jnp.mean(rows * rows, axis=1, keepdims=True) + EPS)


def norm_back(token_rows, recip, gain, grad_normed):
    scaled = grad_normed * gain
    grad_rows = recip * scaled - token_rows * (recip * recip * recip) * jnp.mean(
        scaled * token_rows, axis=1, keepdims=True
    )
    return grad_rows, jnp.sum(grad_normed * token_rows * recip, axis=0, keepdims=True)


def project_kernel(core, own, other, x, cosine, sine, q, kv, n1, qkv_w, out_w, gain_one, gain_two, rows, qkv_b):
    c = core[0]
    for j in range(8):
        rows[c, j * CHUNK : (j + 1) * CHUNK, :] = own[j].astype(F32)[:CHUNK]
        rows[1 - c, j * CHUNK : (j + 1) * CHUNK, :] = other[j].astype(F32)[:CHUNK]
    for t in range(SPAN):
        lanes = tile_at(t)
        gain_one[:, lanes] = rows[0, t : t + 1, :]
        qkv_w[:, lanes] = rows[0, pl.ds(SPAN + t, D, stride=SPAN), :].astype(BF)
        qkv_b[:, lanes] = rows[0, ROW_QB + t : ROW_QB + t + 1, :]
        out_w[:, lanes] = rows[1, pl.ds(ROW_O - HALF + t, D, stride=SPAN), :].astype(BF)
        gain_two[:, lanes] = rows[1, ROW_G2 - HALF + t : ROW_G2 - HALF + t + 1, :]
    qkv_w[:, tile_at(SPAN)] = rows[0, ROW_K : ROW_K + D, :].astype(BF)
    qkv_b[:, tile_at(SPAN)] = rows[0, ROW_KB : ROW_KB + 1, :]
    near = HALF - ROW_V
    value = jnp.concatenate([rows[0, ROW_V:HALF, :], rows[1, : D - near, :]], axis=0)
    qkv_w[:, tile_at(SPAN + 1)] = value.astype(BF)
    qkv_b[:, tile_at(SPAN + 1)] = rows[1, ROW_VB - HALF : ROW_VB - HALF + 1, :]
    n1[...] = (x[...] * recip_rms(x[...]) * gain_one[...]).astype(BF)
    qkv = mm(n1[...], qkv_w[...]) + qkv_b[...]
    for t in range(SPAN):
        q[:, tile_at(t)] = rotate_tile(qkv[:, tile_at(t)], cosine[...], sine[...]).astype(BF)
    kv[:, :LANES] = rotate_tile(qkv[:, tile_at(SPAN)], cosine[...], sine[...]).astype(BF)
    kv[:, LANES:] = qkv[:, tile_at(SPAN + 1)].astype(BF)


def project(core, own, other, x, cosine, sine):
    tokens = x.shape[0]
    return pl.pallas_call(
        project_kernel,
        in_specs=[pl.BlockSpec(memory_space=pltpu.SMEM)] + vmem(5),
        out_specs=vmem(7),
        out_shape=[
            jax.ShapeDtypeStruct((tokens, D), BF),
            jax.ShapeDtypeStruct((tokens, 2 * LANES), BF),
            jax.ShapeDtypeStruct((tokens, D), BF),
            jax.ShapeDtypeStruct((D, QKV), BF),
            jax.ShapeDtypeStruct((D, D), BF),
            jax.ShapeDtypeStruct((1, D), F32),
            jax.ShapeDtypeStruct((1, D), F32),
        ],
        scratch_shapes=[pltpu.VMEM((2, HALF, LANES), F32), pltpu.VMEM((1, QKV), F32)],
        compiler_params=params_of(24),
        cost_estimate=pl.CostEstimate(flops=300 << 20, bytes_accessed=20 << 20, transcendentals=0),
        name="project",
    )(core, own, other, x, cosine, sine)


def pack_kernel(
    core, dqp, n1, x, qkv_w, gain_one, attended, grad_attn, grad_mid, gain_two, cosine, sine, dkv,
    input_grad, mine, theirs, rows, dqkv,
):
    c = core[0]
    total = dkv[0].astype(F32)
    for j in range(1, 8):
        total = total + dkv[j].astype(F32)
    dqkv[:, :D] = dqp[...]
    dqkv[:, tile_at(SPAN)] = rotate_tile(total[:, :LANES], cosine[...], -sine[...]).astype(BF)
    dqkv[:, tile_at(SPAN + 1)] = total[:, LANES:].astype(BF)
    grad_n1 = mm_nt(dqkv[...], qkv_w[...])
    recip = recip_rms(x[...])
    grad_rows, grad_gain = norm_back(x[...], recip, gain_one[...], grad_n1)
    input_grad[...] = grad_mid[...] + grad_rows
    grad = mm_tn(n1[...], dqkv[...])
    bias = jnp.sum(dqkv[...].astype(F32), axis=0, keepdims=True)
    grad_out = mm_tn(attended[...], grad_attn[...])
    for t in range(SPAN):
        lanes = tile_at(t)
        rows[0, t : t + 1, :] = grad_gain[:, lanes]
        rows[0, pl.ds(SPAN + t, D, stride=SPAN), :] = grad[:, lanes]
        rows[0, ROW_QB + t : ROW_QB + t + 1, :] = bias[:, lanes]
        rows[1, pl.ds(ROW_O - HALF + t, D, stride=SPAN), :] = grad_out[:, lanes]
        rows[1, ROW_G2 - HALF + t : ROW_G2 - HALF + t + 1, :] = gain_two[:, lanes]
    rows[0, ROW_K : ROW_K + D, :] = grad[:, tile_at(SPAN)]
    rows[0, ROW_KB : ROW_KB + 1, :] = bias[:, tile_at(SPAN)]
    near = HALF - ROW_V
    rows[0, ROW_V:HALF, :] = grad[:near, tile_at(SPAN + 1)]
    rows[1, : D - near, :] = grad[near:, tile_at(SPAN + 1)]
    rows[1, ROW_VB - HALF : ROW_VB - HALF + 1, :] = bias[:, tile_at(SPAN + 1)]
    rows[1, GU_START - HALF :, :] = jnp.zeros((2 * HALF - GU_START, LANES), F32)
    tail = jnp.zeros((PARTS * PART_ROWS - CHUNK, LANES), F32)
    for j in range(8):
        mine[j] = jnp.concatenate([rows[c, j * CHUNK : (j + 1) * CHUNK, :], tail]).astype(BF)
        theirs[j] = jnp.concatenate([rows[1 - c, j * CHUNK : (j + 1) * CHUNK, :], tail]).astype(BF)


def pack(core, *arrays):
    tokens = arrays[1].shape[0]
    return pl.pallas_call(
        pack_kernel,
        in_specs=[pl.BlockSpec(memory_space=pltpu.SMEM)] + vmem(len(arrays)),
        out_specs=vmem(3),
        out_shape=[
            jax.ShapeDtypeStruct((tokens, D), F32),
            jax.ShapeDtypeStruct((8, PARTS * PART_ROWS, LANES), BF),
            jax.ShapeDtypeStruct((8, PARTS * PART_ROWS, LANES), BF),
        ],
        scratch_shapes=[pltpu.VMEM((2, HALF, LANES), F32), pltpu.VMEM((tokens, QKV), BF)],
        compiler_params=params_of(24),
        cost_estimate=pl.CostEstimate(flops=800 << 20, bytes_accessed=20 << 20, transcendentals=0),
        name="pack",
    )(core, *arrays)


def place_heads(blocks, k_at, v_at):
    kv = blocks[...].reshape(-1, 2 * LANES)
    for source, target in ((kv[:, :LANES], k_at), (kv[:, LANES:], v_at)):
        wide = source.astype(F32)
        low = lax.broadcasted_iota(jnp.int32, wide.shape, 1) < HEAD_DIM
        first, second = jnp.where(low, wide, 0.0), jnp.where(low, 0.0, wide)
        target[0] = first.astype(BF)
        target[1] = pltpu.roll(first, HEAD_DIM, 1).astype(BF)
        target[2] = pltpu.roll(second, HEAD_DIM, 1).astype(BF)
        target[3] = second.astype(BF)


def mark_keys(seg_q, seg_k, place_q, place_k, keep):
    allowed = (seg_q[...] == seg_k[...]) & (place_k[...] <= place_q[...])
    keep[...] = jnp.where(allowed, 1.0, 0.0)


def attend_kernel(
    q, kv, seg_q, seg_k, place_q, place_k, x, out_w, gain_two, attended, lse, mid, n2, k_at, v_at, keep
):
    place_heads(kv, k_at, v_at)
    mark_keys(seg_q, seg_k, place_q, place_k, keep)
    for t in range(SPAN):
        total_out = None
        for half in range(2):
            head = 2 * t + half
            at = (head // GROUP) * 2 + half
            scores = mm_nt(q[:, tile_at(t)], k_at[at]) * (HEAD_DIM**-0.5)
            scores = jnp.where(keep[...] > 0.0, scores, -1e30)
            peak = jnp.max(scores, axis=1, keepdims=True)
            raised = jnp.exp(scores - peak)
            total = jnp.sum(raised, axis=1, keepdims=True)
            shares = (raised * (1.0 / total)).astype(BF)
            part = mm(shares, v_at[at])
            total_out = part if total_out is None else total_out + part
            lse[:, head : head + 1] = peak + jnp.log(total)
        attended[:, tile_at(t)] = total_out.astype(BF)
    mid[...] = x[...] + mm(attended[...], out_w[...])
    n2[...] = (mid[...] * recip_rms(mid[...]) * gain_two[...]).astype(BF)


def attend_back_kernel(
    g0, g1, g2, g3, mid, gain_two, grad_out, out_w, q, kv, lse, seg_q, seg_k, place_q, place_k, cosine, sine,
    grad_mid, grad_attn, dqp, grad_gain, dkv, k_at, v_at, keep, sums,
):
    grad_n2 = g0[...] + g1[...].astype(F32) + g2[...].astype(F32) + g3[...].astype(F32)
    recip = recip_rms(mid[...])
    grad_rows, gain = norm_back(mid[...], recip, gain_two[...], grad_n2)
    grad_gain[...] = gain
    grad_mid[...] = grad_out[...] + grad_rows
    grad_attn[...] = grad_mid[...].astype(BF)
    do = mm_nt(grad_attn[...], out_w[...]).astype(BF)
    place_heads(kv, k_at, v_at)
    mark_keys(seg_q, seg_k, place_q, place_k, keep)
    sums[...] = jnp.zeros_like(sums)
    scale = HEAD_DIM**-0.5
    for t in range(SPAN):
        q_tile, do_tile = q[:, tile_at(t)], do[:, tile_at(t)]
        grad_q = None
        for half in range(2):
            head = 2 * t + half
            group = head // GROUP
            at = group * 2 + half
            scores = mm_nt(q_tile, k_at[at]) * scale
            scores = jnp.where(keep[...] > 0.0, scores, -1e30)
            shares = jnp.exp(scores - lse[:, head : head + 1])
            grad_shares = mm_nt(do_tile, v_at[at])
            delta = jnp.sum(shares * grad_shares, axis=1, keepdims=True)
            grad_scores = (shares * (grad_shares - delta)).astype(BF)
            part = mm(grad_scores, k_at[at])
            grad_q = part if grad_q is None else grad_q + part
            mine = slice(half * HEAD_DIM, (half + 1) * HEAD_DIM)
            sums[group * HEAD_DIM : (group + 1) * HEAD_DIM, :] += mm_tn(q_tile, grad_scores)[mine]
            sums[LANES + group * HEAD_DIM : LANES + (group + 1) * HEAD_DIM, :] += mm_tn(
                do_tile, shares.astype(BF)
            )[mine]
        dqp[:, tile_at(t)] = rotate_tile(grad_q * scale, cosine[...], -sine[...]).astype(BF)
    for j in range(8):
        dkv[j, :, :LANES] = (jnp.transpose(sums[:LANES, tile_at(j)]) * scale).astype(BF)
        dkv[j, :, LANES:] = jnp.transpose(sums[LANES:, tile_at(j)]).astype(BF)


def head_scratch(tokens, length):
    return [
        pltpu.VMEM((4, length, LANES), BF),
        pltpu.VMEM((4, length, LANES), BF),
        pltpu.VMEM((tokens, length), F32),
    ]


def attend(q, kv, masks, x, out_w, gain_two):
    tokens, length = q.shape[0], masks[1].shape[1]
    return pl.pallas_call(
        attend_kernel,
        in_specs=vmem(9),
        out_specs=vmem(4),
        out_shape=[
            jax.ShapeDtypeStruct((tokens, D), BF),
            jax.ShapeDtypeStruct((tokens, 16), F32),
            jax.ShapeDtypeStruct((tokens, D), F32),
            jax.ShapeDtypeStruct((tokens, D), BF),
        ],
        scratch_shapes=head_scratch(tokens, length),
        compiler_params=params_of(24),
        cost_estimate=pl.CostEstimate(
            flops=8 * HEADS * tokens * length * HEAD_DIM,
            bytes_accessed=4 << 20,
            transcendentals=HEADS * tokens * length,
        ),
        name="attend",
    )(q, kv, *masks, x, out_w, gain_two)


def attend_back(grads, mid, gain_two, grad_out, out_w, q, kv, lse, masks, cosine, sine):
    tokens, length = q.shape[0], masks[1].shape[1]
    return pl.pallas_call(
        attend_back_kernel,
        in_specs=vmem(17),
        out_specs=vmem(5),
        out_shape=[
            jax.ShapeDtypeStruct((tokens, D), F32),
            jax.ShapeDtypeStruct((tokens, D), BF),
            jax.ShapeDtypeStruct((tokens, D), BF),
            jax.ShapeDtypeStruct((1, D), F32),
            jax.ShapeDtypeStruct((8, tokens, 2 * LANES), BF),
        ],
        scratch_shapes=head_scratch(tokens, length) + [pltpu.VMEM((2 * LANES, length), F32)],
        compiler_params=params_of(24),
        cost_estimate=pl.CostEstimate(
            flops=20 * HEADS * tokens * length * HEAD_DIM,
            bytes_accessed=8 << 20,
            transcendentals=HEADS * tokens * length,
        ),
        name="attend_back",
    )(*grads, mid, gain_two, grad_out, out_w, q, kv, lse, *masks, cosine, sine)


def mlp_kernel(
    here, x_near, x_far, dy_near, dy_far, gate_w, up_w, down_w,
    y_near, y_far, dx_near, dx_far, low, high, sum_gu, sum_down, stage,
):
    halves = (x_near, dy_near, y_near, dx_near), (x_far, dy_far, y_far, dx_far)
    for first, (x_ref, dy_ref, y_ref, dx_ref) in zip((True, False), halves):
        x, dy = x_ref[...], dy_ref[...]
        gate = mm(x, gate_w[...])
        up = mm(x, up_w[...])
        dh = mm_nt(dy, down_w[...])
        sigmoid = 1.0 / (1.0 + jnp.exp(-gate))
        silu = gate * sigmoid
        hidden = (silu * up).astype(BF)
        dg = (dh * up * sigmoid * (1.0 + gate * (1.0 - sigmoid))).astype(BF)
        du = (dh * silu).astype(BF)
        y_ref[...] = mm(hidden, down_w[...]).astype(BF)
        dx_ref[...] = (mm_nt(dg, gate_w[...]) + mm_nt(du, up_w[...])).astype(BF)
        if first:
            sum_gu[:D, :] = mm_tn(x, dg)
            sum_gu[D:, :] = mm_tn(x, du)
            sum_down[...] = mm_tn(hidden, dy)
        else:
            sum_gu[:D, :] += mm_tn(x, dg)
            sum_gu[D:, :] += mm_tn(x, du)
            sum_down[...] += mm_tn(hidden, dy)
    dissolve(here, sum_gu, sum_down, low, high, stage)


def feed_forward(here, x, dy, gate_w, up_w, down_w):
    tokens = x[0].shape[0]
    sides = jax.ShapeDtypeStruct((tokens, D), BF)
    return pl.pallas_call(
        mlp_kernel,
        in_specs=[pl.BlockSpec(memory_space=pltpu.SMEM)] + vmem(7),
        out_specs=vmem(6),
        out_shape=[
            sides,
            sides,
            sides,
            sides,
            jax.ShapeDtypeStruct((4, 4, MEMBERS, SLOTS // 2, LANES), BF),
            jax.ShapeDtypeStruct((4, 4, MEMBERS, SLOTS // 2, LANES), BF),
        ],
        scratch_shapes=[
            pltpu.VMEM((2 * D, UNITS), F32),
            pltpu.VMEM((UNITS, D), F32),
            pltpu.VMEM((STAGES, SLOTS, LANES), F32),
        ],
        compiler_params=params_of(30),
        cost_estimate=pl.CostEstimate(
            flops=36 * tokens * D * UNITS, bytes_accessed=16 << 20, transcendentals=2 * tokens * UNITS
        ),
        name="feed_forward",
    )(here, *x, *dy, gate_w, up_w, down_w)


def rope_tables(positions):
    half_dim = HEAD_DIM // 2
    freqs = ROPE_BASE ** (-(jnp.arange(half_dim, dtype=F32) * 2.0) / HEAD_DIM)
    angles = positions.astype(F32)[:, None] * freqs
    cosine, sine = jnp.cos(angles), jnp.sin(angles)
    return jnp.concatenate([cosine] * 4, axis=1), jnp.concatenate([-sine, sine] * 2, axis=1)


def spread_near(block):
    return jnp.concatenate([block] + [xor(block, "y", step, 4) for step in range(1, 4)])


def spread(block):
    near = spread_near(block)
    return near, swap(near, "c")


def collect_far(near, far):
    return (near.astype(F32) + swap(far, "c").astype(F32)).reshape(4, -1, D)


def collect_near(total):
    return [total[0]] + [xor(total[step].astype(BF), "y", step, 4) for step in range(1, 4)]


def local(inputs, params, segments, cotangent):
    tokens = inputs.shape[1]
    length = segments.shape[1]
    x = inputs[0]
    grad_out = cotangent[0]
    chunk = lax.axis_index(("z", "xl", "c", "y", "xh"))
    place = lax.axis_index(("y", "xh"))
    core = lax.axis_index("c").astype(jnp.int32).reshape(1)
    here = jnp.stack([lax.axis_index("z"), lax.axis_index(X)]).astype(jnp.int32)

    seg_row = segments[0]
    place_mine = place * tokens + jnp.arange(tokens, dtype=jnp.int32)
    seg_mine = lax.dynamic_slice_in_dim(seg_row, place * tokens, tokens, 0)
    place_keys = jnp.arange(length, dtype=jnp.int32)
    masks = (seg_mine[:, None], seg_row[None, :], place_mine[:, None], place_keys[None, :])
    doc_start = jnp.sum((seg_row[None, :] < seg_mine[:, None]).astype(jnp.int32), axis=1)
    cosine, sine = rope_tables(place_mine - doc_start)

    rows = params.reshape(CHUNK, LANES).astype(BF)
    part = scatter_rows(rows)
    cut = lax.all_to_all(cut_chunk(rows, chunk), ("c", "y"), 0, 0, tiled=True)
    pieces = gather_mlp_near(cut)
    dy = spread(grad_out.astype(BF))
    part, pieces, dy, cosine, sine = lax.optimization_barrier((part, pieces, dy, cosine, sine))
    own = gather_rows(part)
    other = swap(own, "c")
    low, high = gather_mlp_far(*pieces)

    q, kv, normed_one, qkv_w, out_w, gain_one, gain_two = project(core, own, other, x, cosine, sine)
    kv = lax.all_to_all(jnp.broadcast_to(kv[None], (8,) + kv.shape), ("y", "xh"), 0, 0, tiled=True)
    kv, high = lax.optimization_barrier((kv, high))
    attended, lse, mid, normed_two = attend(q, kv, masks, x, out_w, gain_two)
    near, low = lax.optimization_barrier((spread_near(normed_two), low))
    n2 = near, swap(near, "c")
    gate_w, up_w, down_w = assemble(here, (low, high))
    y_near, y_far, dx_near, dx_far, low, high = feed_forward(here, n2, dy, gate_w, up_w, down_w)
    grads = collect_near(collect_far(dx_near, dx_far))
    grads, high = lax.optimization_barrier((grads, high))
    low, high = scatter_mlp_far(low, high)
    grad_mid, grad_attn, dqp, grad_gain_two, dkv = attend_back(
        grads, mid, gain_two, grad_out, out_w, q, kv, lse, masks, cosine, sine
    )
    dkv, y_near, y_far = lax.optimization_barrier((dkv, y_near, y_far))
    dkv = lax.all_to_all(dkv, ("y", "xh"), 0, 0, tiled=True)
    dkv, mlp_part = lax.optimization_barrier((dkv, scatter_mlp_near(low, high)))
    input_grad, mine, theirs = pack(
        core, dqp, normed_one, x, qkv_w, gain_one, attended, grad_attn, grad_mid, grad_gain_two, cosine, sine, dkv
    )
    mlp_grads = lax.all_to_all(mlp_part, ("c", "y"), 0, 0, tiled=True)
    attn_mine = gather_rows_sum(scatter_rows_sum(mine, theirs))
    terms = collect_near(collect_far(y_near, y_far))
    outputs = mid + terms[0] + terms[1].astype(F32) + terms[2].astype(F32) + terms[3].astype(F32)

    gu_mine, is_gu, down_mine, is_down = join_chunk(mlp_grads, chunk)
    flat_row = chunk * CHUNK + jnp.arange(CHUNK, dtype=jnp.int32)[:, None]
    param_grad = jnp.where(flat_row < GU_START, attn_mine, 0.0)
    param_grad = jnp.where(is_gu, gu_mine, param_grad)
    param_grad = jnp.where(is_down, down_mine.astype(F32), param_grad)
    return outputs[None], input_grad[None], param_grad.reshape(-1)


def solution(mesh):
    fine = Mesh(mesh.devices.reshape(4, 2, 2, 4, 2), ("z", "xl", "c", "y", "xh"))
    dp, seq = ("z", "xl", "c"), ("y", "xh")
    placed = (P(dp, seq, None), P(dp + seq), P(dp, None), P(dp, seq, None))
    return jax.shard_map(
        local,
        mesh=fine,
        in_specs=placed,
        out_specs=(P(dp, seq, None), P(dp, seq, None), P(dp + seq)),
        check_vma=False,
    )
```

```python
import functools

import jax
import jax.numpy as jnp
import numpy as np
from jax import lax
from jax.experimental import pallas as pl
from jax.experimental.pallas import tpu as pltpu
from jax.sharding import Mesh, PartitionSpec as P

D = 896
FF = 4864
HEADS = 14
KV_HEADS = 2
HEAD_DIM = 64
GROUP = HEADS // KV_HEADS
EPS = 1e-06
ROPE_BASE = 1000000.0
LANES = 128

CHUNK = 911
TILES = FF // LANES
WIDE = 40
SPAN = D // LANES
Q_ROWS = D * SPAN
GU_START = SPAN + Q_ROWS + SPAN + D + 1 + D + 1 + Q_ROWS + SPAN
GU_ROWS = 2 * D * TILES
DOWN_START = GU_START + GU_ROWS
DOWN_ROWS = FF * SPAN
ATTN_CHUNKS = 16
MEMBERS = 8
UNITS = 640
GU_WIN = 25
DOWN_WIN = 18
SLOTS = 128
DOWN_SLOT = 2
PARTS = 8
PART_ROWS = 120
GU_FIRST, GU_LAST = 15, 90
DOWN_FIRST = 90
MIX_GU = 13
MIX_SKIP = 9

BF = jnp.bfloat16
F32 = jnp.float32


def dot(left, right, dims):
    return lax.dot_general(left, right, (dims, ((), ())), preferred_element_type=F32)


def mm(left, right):
    return dot(left, right, ((1,), (0,)))


def mm_nt(left, right):
    return dot(left, right, ((1,), (1,)))


def mm_tn(left, right):
    return dot(left, right, ((0,), (0,)))


def swap(value, axis):
    return lax.ppermute(value, axis, [(0, 1), (1, 0)])


def xor(value, axis, step, size):
    return lax.ppermute(value, axis, [(i, i ^ step) for i in range(size)])


def scatter_rows(rows):
    parts = jnp.pad(rows, ((0, PARTS * PART_ROWS - CHUNK), (0, 0))).reshape(PARTS, PART_ROWS, LANES)
    return lax.all_to_all(parts, ("xl", "z"), 0, 0, tiled=True)[0]


def gather_rows(part):
    copies = jnp.broadcast_to(part[None], (8 * PARTS, PART_ROWS, LANES))
    own = lax.all_to_all(copies, ("y", "xh", "xl", "z"), 0, 0, tiled=True)
    return own.reshape(8, PARTS * PART_ROWS, LANES)


def scatter_rows_sum(own, other):
    half = (own.astype(F32) + swap(other, "c").astype(F32)).astype(BF)
    half = half.reshape(8 * PARTS, PART_ROWS, LANES)
    half = lax.all_to_all(half, ("y", "xh", "xl", "z"), 0, 0, tiled=True)
    return jnp.sum(half.astype(F32), axis=0)


def gather_rows_sum(part):
    copies = jnp.broadcast_to(part.astype(BF)[None], (PARTS, PART_ROWS, LANES))
    parts = lax.all_to_all(copies, ("xl", "z"), 0, 0, tiled=True)
    return parts.reshape(-1, LANES)[:CHUNK].astype(F32)


def lane_order():
    m = np.arange(8)[:, None]
    lane = np.arange(LANES)[None, :]
    target = (lane % MEMBERS) * LANES + m * 16 + lane // MEMBERS
    return jnp.asarray(target.reshape(-1), jnp.int32)


def lane_matrix():
    target = lane_order()
    return (target[:, None] == jnp.arange(1024, dtype=jnp.int32)[None, :]).astype(BF)


def chunk_places(chunk):
    base = chunk * CHUNK - GU_START
    first = base // TILES
    base_down = chunk * CHUNK - DOWN_START
    first_down = base_down // (MEMBERS * SPAN)
    local = jnp.arange(CHUNK, dtype=jnp.int32)[:, None]
    is_gu = (base + local >= 0) & (base + local < GU_ROWS)
    is_down = (base_down + local >= 0) & (base_down + local < DOWN_ROWS)
    return base - first * TILES, base_down - first_down * MEMBERS * SPAN, is_gu, is_down


def cut_chunk(rows, chunk):
    phase, phase_down, is_gu, is_down = chunk_places(chunk)
    window = jnp.pad(jnp.where(is_gu, rows, 0), ((TILES, TILES + 1), (0, 0)))
    window = lax.dynamic_slice_in_dim(window, TILES - phase, GU_WIN * TILES, 0)
    window = jnp.pad(window.reshape(GU_WIN, TILES, LANES), ((0, 0), (0, WIDE - TILES), (0, 0)))
    window = window.reshape(GU_WIN, 5, 8, LANES).transpose(1, 0, 2, 3).reshape(GU_WIN * 5, 8 * LANES)
    gu = mm(window, lane_matrix()).astype(BF)
    gu = gu.reshape(5, GU_WIN, MEMBERS, LANES).transpose(2, 0, 1, 3)
    group = MEMBERS * SPAN
    window = jnp.pad(jnp.where(is_down, rows, 0), ((group, DOWN_WIN * group - CHUNK), (0, 0)))
    window = lax.dynamic_slice_in_dim(window, group - phase_down, DOWN_WIN * group, 0)
    down = window.reshape(DOWN_WIN, MEMBERS, SPAN, LANES).transpose(1, 2, 0, 3)
    return pack_slots(gu, down, chunk)


def pack_slots(gu, down, chunk):
    flat = gu.reshape(MEMBERS, GU_WIN * 5, LANES), down.reshape(MEMBERS, DOWN_WIN * SPAN, LANES)
    plain = jnp.pad(flat[0], ((0, 0), (0, SLOTS - GU_WIN * 5), (0, 0))) + jnp.pad(
        flat[1], ((0, 0), (DOWN_SLOT, SLOTS - DOWN_SLOT - DOWN_WIN * SPAN), (0, 0))
    )
    mixed = jnp.concatenate(
        [
            gu[:, :, :MIX_GU].reshape(MEMBERS, 5 * MIX_GU, LANES),
            down[:, :, MIX_SKIP : MIX_SKIP + 8].reshape(MEMBERS, 8 * SPAN, LANES),
        ],
        axis=1,
    )
    mixed = jnp.pad(mixed, ((0, 0), (0, SLOTS - 5 * MIX_GU - 8 * SPAN), (0, 0)))
    return jnp.where(chunk == DOWN_FIRST, mixed, plain)


def join_chunk(cut, chunk):
    phase, phase_down, is_gu, is_down = chunk_places(chunk)
    gu = cut[:, : GU_WIN * 5].reshape(MEMBERS, 5, GU_WIN, LANES)
    mixed = cut[:, : 5 * MIX_GU].reshape(MEMBERS, 5, MIX_GU, LANES)
    mixed = jnp.pad(mixed, ((0, 0), (0, 0), (0, GU_WIN - MIX_GU), (0, 0)))
    gu = jnp.where(chunk == DOWN_FIRST, mixed, gu)
    gu = gu.transpose(1, 2, 0, 3).reshape(GU_WIN * 5, MEMBERS * LANES)
    gu = mm_nt(gu, lane_matrix())
    gu = gu.reshape(5, GU_WIN, 8, LANES).transpose(1, 0, 2, 3).reshape(GU_WIN, WIDE, LANES)
    gu = gu[:, :TILES].reshape(GU_WIN * TILES, LANES)
    gu = lax.dynamic_slice_in_dim(gu, phase, CHUNK, 0)
    down = cut[:, DOWN_SLOT : DOWN_SLOT + DOWN_WIN * SPAN].reshape(MEMBERS, SPAN, DOWN_WIN, LANES)
    mixed = cut[:, 5 * MIX_GU : 5 * MIX_GU + 8 * SPAN].reshape(MEMBERS, SPAN, 8, LANES)
    mixed = jnp.pad(mixed, ((0, 0), (0, 0), (MIX_SKIP, DOWN_WIN - MIX_SKIP - 8), (0, 0)))
    down = jnp.where(chunk == DOWN_FIRST, mixed, down).transpose(2, 0, 1, 3)
    down = down.reshape(DOWN_WIN * MEMBERS * SPAN, LANES)
    down = lax.dynamic_slice_in_dim(down, phase_down, CHUNK, 0)
    return gu, is_gu, down, is_down


X = ("xl", "xh")


def ring_blocks(block, axis):
    return [block] + [xor(block, axis, step, 4) for step in range(1, 4)]


def ring_gather(block, axis):
    return jnp.stack(ring_blocks(block, axis))


def ring_sum(blocks, axis):
    total = blocks[0].astype(F32)
    for step in range(1, 4):
        total = total + xor(blocks[step], axis, step, 4).astype(F32)
    return total.astype(BF)


def gather_mlp_near(cut):
    low = jnp.broadcast_to(cut[None, :, : SLOTS // 2], (4, MEMBERS, SLOTS // 2, LANES))
    return lax.all_to_all(low, "z", 0, 0, tiled=True), ring_gather(cut[:, SLOTS // 2 :], X)


def gather_mlp_far(low, high):
    return ring_gather(low, X), ring_blocks(high, "z")


def scatter_mlp_far(low, high):
    low = lax.all_to_all(low, "z", 0, 0, tiled=True)
    return jnp.sum(low.astype(F32), axis=0).astype(BF), ring_sum(high, X)


def scatter_mlp_near(low, high):
    return jnp.concatenate([ring_sum(low, X), ring_sum(high, "z")], axis=1)


def chunk_index(chunk):
    return chunk >> 5, ((chunk >> 4) & 1) * 2 + (chunk & 1), (chunk >> 1) & 7


def gu_moves(chunk):
    start = (chunk * CHUNK - GU_START) // TILES
    step = MIX_GU if chunk == DOWN_FIRST else GU_WIN
    moves = []
    for side in range(2):
        low, high = max(0, side * D - start), min(GU_WIN, (side + 1) * D - start)
        for j in range(5 if low < high else 0):
            moves.append((j * step + low, start + low - side * D, high - low, side * UNITS + j * LANES))
    return moves


def down_moves(chunk):
    start = (chunk * CHUNK - DOWN_START) // (MEMBERS * SPAN)
    if chunk == DOWN_FIRST:
        return [(5 * MIX_GU + c * 8, 0, 8, c * LANES) for c in range(SPAN)]
    high = min(DOWN_WIN, UNITS - start)
    return [(DOWN_SLOT + c * DOWN_WIN, start, high, c * LANES) for c in range(SPAN)]


STAGES = 4


def assemble_kernel(here, low, high, gu_w, down_w, stage, gu_sum, down_sum):
    gu_sum[...] = jnp.zeros_like(gu_sum)
    down_sum[...] = jnp.zeros_like(down_sum)
    for chunk in range(GU_FIRST, 128):
        slot = stage.at[chunk % STAGES]
        z, x, member = chunk_index(chunk)
        slot[: SLOTS // 2, :] = low[here[1] ^ x, z, member].astype(F32)
        slot[SLOTS // 2 :, :] = high[here[0] ^ z, here[1] ^ x, member].astype(F32)
        if chunk <= GU_LAST:
            for at, row, count, lane in gu_moves(chunk):
                gu_sum[row : row + count, lane : lane + LANES] += slot[at : at + count, :]
        if chunk >= DOWN_FIRST:
            for at, row, count, lane in down_moves(chunk):
                down_sum[row : row + count, lane : lane + LANES] += slot[at : at + count, :]
    gu_w[...] = gu_sum[...].astype(BF)
    down_w[...] = down_sum[...].astype(BF)


def dissolve(here, gu, down, low, high, stage):
    stage[...] = jnp.zeros_like(stage)
    for chunk in range(128):
        chunk_z, x, member = chunk_index(chunk)
        z, x = here[0] ^ chunk_z, here[1] ^ x
        if chunk < GU_FIRST:
            low[chunk_z, x, member] = jnp.zeros((SLOTS // 2, LANES), BF)
            high[x, z, member] = jnp.zeros((SLOTS // 2, LANES), BF)
            continue
        slot = stage.at[chunk % STAGES]
        if chunk <= GU_LAST:
            for at, row, count, lane in gu_moves(chunk):
                slot[at : at + count, :] = gu[row : row + count, lane : lane + LANES]
        if chunk >= DOWN_FIRST:
            for at, row, count, lane in down_moves(chunk):
                slot[at : at + count, :] = down[row : row + count, lane : lane + LANES]
        low[chunk_z, x, member] = slot[: SLOTS // 2, :].astype(BF)
        high[x, z, member] = slot[SLOTS // 2 :, :].astype(BF)


def vmem(count):
    return [pl.BlockSpec(memory_space=pltpu.VMEM)] * count


def params_of(megabytes):
    return pltpu.CompilerParams(vmem_limit_bytes=megabytes << 20)


def assemble(here, pieces):
    return pl.pallas_call(
        assemble_kernel,
        in_specs=[pl.BlockSpec(memory_space=pltpu.SMEM)] + vmem(2),
        out_specs=vmem(2),
        out_shape=[
            jax.ShapeDtypeStruct((D, 2 * UNITS), BF),
            jax.ShapeDtypeStruct((UNITS, D), BF),
        ],
        scratch_shapes=[
            pltpu.VMEM((STAGES, SLOTS, LANES), F32),
            pltpu.VMEM((D, 2 * UNITS), F32),
            pltpu.VMEM((UNITS, D), F32),
        ],
        compiler_params=params_of(24),
        cost_estimate=pl.CostEstimate(flops=10 << 20, bytes_accessed=20 << 20, transcendentals=0),
        name="assemble",
    )(here, *pieces)


HALF = 8 * CHUNK
ROW_QB = SPAN + Q_ROWS
ROW_K = ROW_QB + SPAN
ROW_KB = ROW_K + D
ROW_V = ROW_KB + 1
ROW_VB = ROW_V + D
ROW_O = ROW_VB + 1
ROW_G2 = ROW_O + Q_ROWS
QKV = D + 2 * LANES


def rotate_tile(tile, cosine, sine):
    half_dim = HEAD_DIM // 2
    lane = lax.broadcasted_iota(jnp.int32, tile.shape, 1)
    other = jnp.where(
        lane % HEAD_DIM < half_dim,
        pltpu.roll(tile, LANES - half_dim, 1),
        pltpu.roll(tile, half_dim, 1),
    )
    return tile * cosine + other * sine


def tile_at(t):
    return slice(t * LANES, (t + 1) * LANES)


def recip_rms(rows):
    return lax.rsqrt(jnp.mean(rows * rows, axis=1, keepdims=True) + EPS)


def norm_back(token_rows, recip, gain, grad_normed):
    scaled = grad_normed * gain
    grad_rows = recip * scaled - token_rows * (recip * recip * recip) * jnp.mean(
        scaled * token_rows, axis=1, keepdims=True
    )
    return grad_rows, jnp.sum(grad_normed * token_rows * recip, axis=0, keepdims=True)


def project_kernel(core, own, other, x, cosine, sine, q, kv, n1, qkv_w, out_w, gain_one, gain_two, rows, qkv_b):
    c = core[0]
    for j in range(8):
        rows[c, j * CHUNK : (j + 1) * CHUNK, :] = own[j].astype(F32)[:CHUNK]
        rows[1 - c, j * CHUNK : (j + 1) * CHUNK, :] = other[j].astype(F32)[:CHUNK]
    for t in range(SPAN):
        lanes = tile_at(t)
        gain_one[:, lanes] = rows[0, t : t + 1, :]
        qkv_w[:, lanes] = rows[0, pl.ds(SPAN + t, D, stride=SPAN), :].astype(BF)
        qkv_b[:, lanes] = rows[0, ROW_QB + t : ROW_QB + t + 1, :]
        out_w[:, lanes] = rows[1, pl.ds(ROW_O - HALF + t, D, stride=SPAN), :].astype(BF)
        gain_two[:, lanes] = rows[1, ROW_G2 - HALF + t : ROW_G2 - HALF + t + 1, :]
    qkv_w[:, tile_at(SPAN)] = rows[0, ROW_K : ROW_K + D, :].astype(BF)
    qkv_b[:, tile_at(SPAN)] = rows[0, ROW_KB : ROW_KB + 1, :]
    near = HALF - ROW_V
    value = jnp.concatenate([rows[0, ROW_V:HALF, :], rows[1, : D - near, :]], axis=0)
    qkv_w[:, tile_at(SPAN + 1)] = value.astype(BF)
    qkv_b[:, tile_at(SPAN + 1)] = rows[1, ROW_VB - HALF : ROW_VB - HALF + 1, :]
    n1[...] = (x[...] * recip_rms(x[...]) * gain_one[...]).astype(BF)
    qkv = mm(n1[...], qkv_w[...]) + qkv_b[...]
    for t in range(SPAN):
        q[:, tile_at(t)] = rotate_tile(qkv[:, tile_at(t)], cosine[...], sine[...]).astype(BF)
    kv[:, :LANES] = rotate_tile(qkv[:, tile_at(SPAN)], cosine[...], sine[...]).astype(BF)
    kv[:, LANES:] = qkv[:, tile_at(SPAN + 1)].astype(BF)


def project(core, own, other, x, cosine, sine):
    tokens = x.shape[0]
    return pl.pallas_call(
        project_kernel,
        in_specs=[pl.BlockSpec(memory_space=pltpu.SMEM)] + vmem(5),
        out_specs=vmem(7),
        out_shape=[
            jax.ShapeDtypeStruct((tokens, D), BF),
            jax.ShapeDtypeStruct((tokens, 2 * LANES), BF),
            jax.ShapeDtypeStruct((tokens, D), BF),
            jax.ShapeDtypeStruct((D, QKV), BF),
            jax.ShapeDtypeStruct((D, D), BF),
            jax.ShapeDtypeStruct((1, D), F32),
            jax.ShapeDtypeStruct((1, D), F32),
        ],
        scratch_shapes=[pltpu.VMEM((2, HALF, LANES), F32), pltpu.VMEM((1, QKV), F32)],
        compiler_params=params_of(24),
        cost_estimate=pl.CostEstimate(flops=300 << 20, bytes_accessed=20 << 20, transcendentals=0),
        name="project",
    )(core, own, other, x, cosine, sine)


def pack_kernel(
    core, dqp, n1, x, qkv_w, gain_one, attended, grad_attn, grad_mid, gain_two, cosine, sine, dkv,
    input_grad, mine, theirs, rows, dqkv,
):
    c = core[0]
    total = dkv[0].astype(F32)
    for j in range(1, 8):
        total = total + dkv[j].astype(F32)
    dqkv[:, :D] = dqp[...]
    dqkv[:, tile_at(SPAN)] = rotate_tile(total[:, :LANES], cosine[...], -sine[...]).astype(BF)
    dqkv[:, tile_at(SPAN + 1)] = total[:, LANES:].astype(BF)
    grad_n1 = mm_nt(dqkv[...], qkv_w[...])
    recip = recip_rms(x[...])
    grad_rows, grad_gain = norm_back(x[...], recip, gain_one[...], grad_n1)
    input_grad[...] = grad_mid[...] + grad_rows
    grad = mm_tn(n1[...], dqkv[...])
    bias = jnp.sum(dqkv[...].astype(F32), axis=0, keepdims=True)
    grad_out = mm_tn(attended[...], grad_attn[...])
    for t in range(SPAN):
        lanes = tile_at(t)
        rows[0, t : t + 1, :] = grad_gain[:, lanes]
        rows[0, pl.ds(SPAN + t, D, stride=SPAN), :] = grad[:, lanes]
        rows[0, ROW_QB + t : ROW_QB + t + 1, :] = bias[:, lanes]
        rows[1, pl.ds(ROW_O - HALF + t, D, stride=SPAN), :] = grad_out[:, lanes]
        rows[1, ROW_G2 - HALF + t : ROW_G2 - HALF + t + 1, :] = gain_two[:, lanes]
    rows[0, ROW_K : ROW_K + D, :] = grad[:, tile_at(SPAN)]
    rows[0, ROW_KB : ROW_KB + 1, :] = bias[:, tile_at(SPAN)]
    near = HALF - ROW_V
    rows[0, ROW_V:HALF, :] = grad[:near, tile_at(SPAN + 1)]
    rows[1, : D - near, :] = grad[near:, tile_at(SPAN + 1)]
    rows[1, ROW_VB - HALF : ROW_VB - HALF + 1, :] = bias[:, tile_at(SPAN + 1)]
    rows[1, GU_START - HALF :, :] = jnp.zeros((2 * HALF - GU_START, LANES), F32)
    tail = jnp.zeros((PARTS * PART_ROWS - CHUNK, LANES), F32)
    for j in range(8):
        mine[j] = jnp.concatenate([rows[c, j * CHUNK : (j + 1) * CHUNK, :], tail]).astype(BF)
        theirs[j] = jnp.concatenate([rows[1 - c, j * CHUNK : (j + 1) * CHUNK, :], tail]).astype(BF)


def pack(core, *arrays):
    tokens = arrays[1].shape[0]
    return pl.pallas_call(
        pack_kernel,
        in_specs=[pl.BlockSpec(memory_space=pltpu.SMEM)] + vmem(len(arrays)),
        out_specs=vmem(3),
        out_shape=[
            jax.ShapeDtypeStruct((tokens, D), F32),
            jax.ShapeDtypeStruct((8, PARTS * PART_ROWS, LANES), BF),
            jax.ShapeDtypeStruct((8, PARTS * PART_ROWS, LANES), BF),
        ],
        scratch_shapes=[pltpu.VMEM((2, HALF, LANES), F32), pltpu.VMEM((tokens, QKV), BF)],
        compiler_params=params_of(24),
        cost_estimate=pl.CostEstimate(flops=800 << 20, bytes_accessed=20 << 20, transcendentals=0),
        name="pack",
    )(core, *arrays)


def place_heads(blocks, k_at, v_at):
    kv = blocks[...].reshape(-1, 2 * LANES)
    for source, target in ((kv[:, :LANES], k_at), (kv[:, LANES:], v_at)):
        wide = source.astype(F32)
        low = lax.broadcasted_iota(jnp.int32, wide.shape, 1) < HEAD_DIM
        first, second = jnp.where(low, wide, 0.0), jnp.where(low, 0.0, wide)
        target[0] = first.astype(BF)
        target[1] = pltpu.roll(first, HEAD_DIM, 1).astype(BF)
        target[2] = pltpu.roll(second, HEAD_DIM, 1).astype(BF)
        target[3] = second.astype(BF)


def mark_keys(seg_q, seg_k, place_q, place_k, keep):
    allowed = (seg_q[...] == seg_k[...]) & (place_k[...] <= place_q[...])
    keep[...] = jnp.where(allowed, 1.0, 0.0)


def attend_kernel(
    q, kv, seg_q, seg_k, place_q, place_k, x, out_w, gain_two, attended, lse, mid, n2, k_at, v_at, keep
):
    place_heads(kv, k_at, v_at)
    mark_keys(seg_q, seg_k, place_q, place_k, keep)
    for t in range(SPAN):
        total_out = None
        for half in range(2):
            head = 2 * t + half
            at = (head // GROUP) * 2 + half
            scores = mm_nt(q[:, tile_at(t)], k_at[at]) * (HEAD_DIM**-0.5)
            scores = jnp.where(keep[...] > 0.0, scores, -1e30)
            peak = jnp.max(scores, axis=1, keepdims=True)
            raised = jnp.exp(scores - peak)
            total = jnp.sum(raised, axis=1, keepdims=True)
            shares = (raised * (1.0 / total)).astype(BF)
            part = mm(shares, v_at[at])
            total_out = part if total_out is None else total_out + part
            lse[:, head : head + 1] = peak + jnp.log(total)
        attended[:, tile_at(t)] = total_out.astype(BF)
    mid[...] = x[...] + mm(attended[...], out_w[...])
    n2[...] = (mid[...] * recip_rms(mid[...]) * gain_two[...]).astype(BF)


def attend_back_kernel(
    g0, g1, g2, g3, mid, gain_two, grad_out, out_w, q, kv, lse, seg_q, seg_k, place_q, place_k, cosine, sine,
    grad_mid, grad_attn, dqp, grad_gain, dkv, k_at, v_at, keep, sums,
):
    grad_n2 = g0[...] + g1[...].astype(F32) + g2[...].astype(F32) + g3[...].astype(F32)
    recip = recip_rms(mid[...])
    grad_rows, gain = norm_back(mid[...], recip, gain_two[...], grad_n2)
    grad_gain[...] = gain
    grad_mid[...] = grad_out[...] + grad_rows
    grad_attn[...] = grad_mid[...].astype(BF)
    do = mm_nt(grad_attn[...], out_w[...]).astype(BF)
    place_heads(kv, k_at, v_at)
    mark_keys(seg_q, seg_k, place_q, place_k, keep)
    sums[...] = jnp.zeros_like(sums)
    scale = HEAD_DIM**-0.5
    for t in range(SPAN):
        q_tile, do_tile = q[:, tile_at(t)], do[:, tile_at(t)]
        grad_q = None
        for half in range(2):
            head = 2 * t + half
            group = head // GROUP
            at = group * 2 + half
            scores = mm_nt(q_tile, k_at[at]) * scale
            scores = jnp.where(keep[...] > 0.0, scores, -1e30)
            shares = jnp.exp(scores - lse[:, head : head + 1])
            grad_shares = mm_nt(do_tile, v_at[at])
            delta = jnp.sum(shares * grad_shares, axis=1, keepdims=True)
            grad_scores = (shares * (grad_shares - delta)).astype(BF)
            part = mm(grad_scores, k_at[at])
            grad_q = part if grad_q is None else grad_q + part
            mine = slice(half * HEAD_DIM, (half + 1) * HEAD_DIM)
            sums[group * HEAD_DIM : (group + 1) * HEAD_DIM, :] += mm_tn(q_tile, grad_scores)[mine]
            sums[LANES + group * HEAD_DIM : LANES + (group + 1) * HEAD_DIM, :] += mm_tn(
                do_tile, shares.astype(BF)
            )[mine]
        dqp[:, tile_at(t)] = rotate_tile(grad_q * scale, cosine[...], -sine[...]).astype(BF)
    for j in range(8):
        dkv[j, :, :LANES] = (jnp.transpose(sums[:LANES, tile_at(j)]) * scale).astype(BF)
        dkv[j, :, LANES:] = jnp.transpose(sums[LANES:, tile_at(j)]).astype(BF)


def head_scratch(tokens, length):
    return [
        pltpu.VMEM((4, length, LANES), BF),
        pltpu.VMEM((4, length, LANES), BF),
        pltpu.VMEM((tokens, length), F32),
    ]


def attend(q, kv, masks, x, out_w, gain_two):
    tokens, length = q.shape[0], masks[1].shape[1]
    return pl.pallas_call(
        attend_kernel,
        in_specs=vmem(9),
        out_specs=vmem(4),
        out_shape=[
            jax.ShapeDtypeStruct((tokens, D), BF),
            jax.ShapeDtypeStruct((tokens, 16), F32),
            jax.ShapeDtypeStruct((tokens, D), F32),
            jax.ShapeDtypeStruct((tokens, D), BF),
        ],
        scratch_shapes=head_scratch(tokens, length),
        compiler_params=params_of(24),
        cost_estimate=pl.CostEstimate(
            flops=8 * HEADS * tokens * length * HEAD_DIM,
            bytes_accessed=4 << 20,
            transcendentals=HEADS * tokens * length,
        ),
        name="attend",
    )(q, kv, *masks, x, out_w, gain_two)


def attend_back(grads, mid, gain_two, grad_out, out_w, q, kv, lse, masks, cosine, sine):
    tokens, length = q.shape[0], masks[1].shape[1]
    return pl.pallas_call(
        attend_back_kernel,
        in_specs=vmem(17),
        out_specs=vmem(5),
        out_shape=[
            jax.ShapeDtypeStruct((tokens, D), F32),
            jax.ShapeDtypeStruct((tokens, D), BF),
            jax.ShapeDtypeStruct((tokens, D), BF),
            jax.ShapeDtypeStruct((1, D), F32),
            jax.ShapeDtypeStruct((8, tokens, 2 * LANES), BF),
        ],
        scratch_shapes=head_scratch(tokens, length) + [pltpu.VMEM((2 * LANES, length), F32)],
        compiler_params=params_of(24),
        cost_estimate=pl.CostEstimate(
            flops=20 * HEADS * tokens * length * HEAD_DIM,
            bytes_accessed=8 << 20,
            transcendentals=HEADS * tokens * length,
        ),
        name="attend_back",
    )(*grads, mid, gain_two, grad_out, out_w, q, kv, lse, *masks, cosine, sine)


def mlp_kernel(
    here, x_near, x_far, dy_near, dy_far, gu_w, down_w,
    y_near, y_far, dx_near, dx_far, low, high, sum_gu, sum_down, stage,
):
    halves = (x_near, dy_near, y_near, dx_near), (x_far, dy_far, y_far, dx_far)
    for first, (x_ref, dy_ref, y_ref, dx_ref) in zip((True, False), halves):
        x, dy = x_ref[...], dy_ref[...]
        both = mm(x, gu_w[...])
        gate, up = both[:, :UNITS], both[:, UNITS:]
        dh = mm_nt(dy, down_w[...])
        sigmoid = 1.0 / (1.0 + jnp.exp(-gate))
        silu = gate * sigmoid
        hidden = (silu * up).astype(BF)
        dg = (dh * up * sigmoid * (1.0 + gate * (1.0 - sigmoid))).astype(BF)
        du = (dh * silu).astype(BF)
        y_ref[...] = mm(hidden, down_w[...]).astype(BF)
        both = jnp.concatenate([dg, du], axis=1)
        dx_ref[...] = mm_nt(both, gu_w[...]).astype(BF)
        if first:
            sum_gu[...] = mm_tn(x, both)
            sum_down[...] = mm_tn(hidden, dy)
        else:
            sum_gu[...] += mm_tn(x, both)
            sum_down[...] += mm_tn(hidden, dy)
    dissolve(here, sum_gu, sum_down, low, high, stage)


def feed_forward(here, x, dy, gu_w, down_w):
    tokens = x[0].shape[0]
    sides = jax.ShapeDtypeStruct((tokens, D), BF)
    return pl.pallas_call(
        mlp_kernel,
        in_specs=[pl.BlockSpec(memory_space=pltpu.SMEM)] + vmem(6),
        out_specs=vmem(6),
        out_shape=[
            sides,
            sides,
            sides,
            sides,
            jax.ShapeDtypeStruct((4, 4, MEMBERS, SLOTS // 2, LANES), BF),
            jax.ShapeDtypeStruct((4, 4, MEMBERS, SLOTS // 2, LANES), BF),
        ],
        scratch_shapes=[
            pltpu.VMEM((D, 2 * UNITS), F32),
            pltpu.VMEM((UNITS, D), F32),
            pltpu.VMEM((STAGES, SLOTS, LANES), F32),
        ],
        compiler_params=params_of(30),
        cost_estimate=pl.CostEstimate(
            flops=36 * tokens * D * UNITS, bytes_accessed=16 << 20, transcendentals=2 * tokens * UNITS
        ),
        name="feed_forward",
    )(here, *x, *dy, gu_w, down_w)


def rope_tables(positions):
    half_dim = HEAD_DIM // 2
    freqs = ROPE_BASE ** (-(jnp.arange(half_dim, dtype=F32) * 2.0) / HEAD_DIM)
    angles = positions.astype(F32)[:, None] * freqs
    cosine, sine = jnp.cos(angles), jnp.sin(angles)
    return jnp.concatenate([cosine] * 4, axis=1), jnp.concatenate([-sine, sine] * 2, axis=1)


def spread_near(block):
    return jnp.concatenate([block] + [xor(block, "y", step, 4) for step in range(1, 4)])


def spread(block):
    near = spread_near(block)
    return near, swap(near, "c")


def collect_far(near, far):
    return (near.astype(F32) + swap(far, "c").astype(F32)).reshape(4, -1, D)


def collect_near(total):
    return [total[0]] + [xor(total[step].astype(BF), "y", step, 4) for step in range(1, 4)]


def local(inputs, params, segments, cotangent):
    tokens = inputs.shape[1]
    length = segments.shape[1]
    x = inputs[0]
    grad_out = cotangent[0]
    chunk = lax.axis_index(("z", "xl", "c", "y", "xh"))
    place = lax.axis_index(("y", "xh"))
    core = lax.axis_index("c").astype(jnp.int32).reshape(1)
    here = jnp.stack([lax.axis_index("z"), lax.axis_index(X)]).astype(jnp.int32)

    seg_row = segments[0]
    place_mine = place * tokens + jnp.arange(tokens, dtype=jnp.int32)
    seg_mine = lax.dynamic_slice_in_dim(seg_row, place * tokens, tokens, 0)
    place_keys = jnp.arange(length, dtype=jnp.int32)
    masks = (seg_mine[:, None], seg_row[None, :], place_mine[:, None], place_keys[None, :])
    doc_start = jnp.sum((seg_row[None, :] < seg_mine[:, None]).astype(jnp.int32), axis=1)
    cosine, sine = rope_tables(place_mine - doc_start)

    rows = params.reshape(CHUNK, LANES).astype(BF)
    part = scatter_rows(rows)
    cut = lax.all_to_all(cut_chunk(rows, chunk), ("c", "y"), 0, 0, tiled=True)
    pieces = gather_mlp_near(cut)
    dy = spread(grad_out.astype(BF))
    part, pieces, dy, cosine, sine = lax.optimization_barrier((part, pieces, dy, cosine, sine))
    own = gather_rows(part)
    other = swap(own, "c")
    low, high = gather_mlp_far(*pieces)

    q, kv, normed_one, qkv_w, out_w, gain_one, gain_two = project(core, own, other, x, cosine, sine)
    kv = lax.all_to_all(jnp.broadcast_to(kv[None], (8,) + kv.shape), ("y", "xh"), 0, 0, tiled=True)
    kv, high = lax.optimization_barrier((kv, high))
    attended, lse, mid, normed_two = attend(q, kv, masks, x, out_w, gain_two)
    near, low = lax.optimization_barrier((spread_near(normed_two), low))
    n2 = near, swap(near, "c")
    gu_w, down_w = assemble(here, (low, jnp.stack(high)))
    y_near, y_far, dx_near, dx_far, low, high = feed_forward(here, n2, dy, gu_w, down_w)
    grads = collect_near(collect_far(dx_near, dx_far))
    grads, high = lax.optimization_barrier((grads, high))
    low, high = scatter_mlp_far(low, high)
    grad_mid, grad_attn, dqp, grad_gain_two, dkv = attend_back(
        grads, mid, gain_two, grad_out, out_w, q, kv, lse, masks, cosine, sine
    )
    dkv, y_near, y_far = lax.optimization_barrier((dkv, y_near, y_far))
    dkv = lax.all_to_all(dkv, ("y", "xh"), 0, 0, tiled=True)
    dkv, mlp_part = lax.optimization_barrier((dkv, scatter_mlp_near(low, high)))
    input_grad, mine, theirs = pack(
        core, dqp, normed_one, x, qkv_w, gain_one, attended, grad_attn, grad_mid, grad_gain_two, cosine, sine, dkv
    )
    mlp_grads = lax.all_to_all(mlp_part, ("c", "y"), 0, 0, tiled=True)
    attn_mine = gather_rows_sum(scatter_rows_sum(mine, theirs))
    terms = collect_near(collect_far(y_near, y_far))
    outputs = mid + terms[0] + terms[1].astype(F32) + terms[2].astype(F32) + terms[3].astype(F32)

    gu_mine, is_gu, down_mine, is_down = join_chunk(mlp_grads, chunk)
    flat_row = chunk * CHUNK + jnp.arange(CHUNK, dtype=jnp.int32)[:, None]
    param_grad = jnp.where(flat_row < GU_START, attn_mine, 0.0)
    param_grad = jnp.where(is_gu, gu_mine, param_grad)
    param_grad = jnp.where(is_down, down_mine.astype(F32), param_grad)
    return outputs[None], input_grad[None], param_grad.reshape(-1)


def solution(mesh):
    fine = Mesh(mesh.devices.reshape(4, 2, 2, 4, 2), ("z", "xl", "c", "y", "xh"))
    dp, seq = ("z", "xl", "c"), ("y", "xh")
    placed = (P(dp, seq, None), P(dp + seq), P(dp, None), P(dp, seq, None))
    return jax.shard_map(
        local,
        mesh=fine,
        in_specs=placed,
        out_specs=(P(dp, seq, None), P(dp, seq, None), P(dp + seq)),
        check_vma=False,
    )
```

```python
import functools

import jax
import jax.numpy as jnp
import numpy as np
from jax import lax
from jax.experimental import pallas as pl
from jax.experimental.pallas import tpu as pltpu
from jax.sharding import Mesh, PartitionSpec as P

D = 896
FF = 4864
HEADS = 14
KV_HEADS = 2
HEAD_DIM = 64
GROUP = HEADS // KV_HEADS
EPS = 1e-06
ROPE_BASE = 1000000.0
LANES = 128

CHUNK = 911
TILES = FF // LANES
WIDE = 40
SPAN = D // LANES
Q_ROWS = D * SPAN
GU_START = SPAN + Q_ROWS + SPAN + D + 1 + D + 1 + Q_ROWS + SPAN
GU_ROWS = 2 * D * TILES
DOWN_START = GU_START + GU_ROWS
DOWN_ROWS = FF * SPAN
ATTN_CHUNKS = 16
MEMBERS = 8
UNITS = 640
GU_WIN = 25
DOWN_WIN = 18
SLOTS = 128
DOWN_SLOT = 2
PARTS = 8
PART_ROWS = 120
GU_FIRST, GU_LAST = 15, 90
DOWN_FIRST = 90
MIX_GU = 13
MIX_SKIP = 9

BF = jnp.bfloat16
F32 = jnp.float32


def dot(left, right, dims):
    return lax.dot_general(left, right, (dims, ((), ())), preferred_element_type=F32)


def mm(left, right):
    return dot(left, right, ((1,), (0,)))


def mm_nt(left, right):
    return dot(left, right, ((1,), (1,)))


def mm_tn(left, right):
    return dot(left, right, ((0,), (0,)))


def swap(value, axis):
    return lax.ppermute(value, axis, [(0, 1), (1, 0)])


def xor(value, axis, step, size):
    return lax.ppermute(value, axis, [(i, i ^ step) for i in range(size)])


def scatter_rows(rows):
    parts = jnp.pad(rows, ((0, PARTS * PART_ROWS - CHUNK), (0, 0))).reshape(PARTS, PART_ROWS, LANES)
    return lax.all_to_all(parts, ("xl", "z"), 0, 0, tiled=True)[0]


def gather_rows(part):
    copies = jnp.broadcast_to(part[None], (8 * PARTS, PART_ROWS, LANES))
    own = lax.all_to_all(copies, ("y", "xh", "xl", "z"), 0, 0, tiled=True)
    return own.reshape(8, PARTS * PART_ROWS, LANES)


def scatter_rows_sum(own, other):
    half = (own.astype(F32) + swap(other, "c").astype(F32)).astype(BF)
    half = half.reshape(8 * PARTS, PART_ROWS, LANES)
    half = lax.all_to_all(half, ("y", "xh", "xl", "z"), 0, 0, tiled=True)
    return jnp.sum(half.astype(F32), axis=0)


def gather_rows_sum(part):
    copies = jnp.broadcast_to(part.astype(BF)[None], (PARTS, PART_ROWS, LANES))
    parts = lax.all_to_all(copies, ("xl", "z"), 0, 0, tiled=True)
    return parts.reshape(-1, LANES)[:CHUNK].astype(F32)


def lane_order():
    m = np.arange(8)[:, None]
    lane = np.arange(LANES)[None, :]
    target = (lane % MEMBERS) * LANES + m * 16 + lane // MEMBERS
    return jnp.asarray(target.reshape(-1), jnp.int32)


def lane_matrix():
    target = lane_order()
    return (target[:, None] == jnp.arange(1024, dtype=jnp.int32)[None, :]).astype(BF)


def chunk_places(chunk):
    base = chunk * CHUNK - GU_START
    first = base // TILES
    base_down = chunk * CHUNK - DOWN_START
    first_down = base_down // (MEMBERS * SPAN)
    local = jnp.arange(CHUNK, dtype=jnp.int32)[:, None]
    is_gu = (base + local >= 0) & (base + local < GU_ROWS)
    is_down = (base_down + local >= 0) & (base_down + local < DOWN_ROWS)
    return base - first * TILES, base_down - first_down * MEMBERS * SPAN, is_gu, is_down


def cut_chunk(rows, chunk):
    phase, phase_down, is_gu, is_down = chunk_places(chunk)
    window = jnp.pad(jnp.where(is_gu, rows, 0), ((TILES, TILES + 1), (0, 0)))
    window = lax.dynamic_slice_in_dim(window, TILES - phase, GU_WIN * TILES, 0)
    window = jnp.pad(window.reshape(GU_WIN, TILES, LANES), ((0, 0), (0, WIDE - TILES), (0, 0)))
    window = window.reshape(GU_WIN, 5, 8, LANES).transpose(1, 0, 2, 3).reshape(GU_WIN * 5, 8 * LANES)
    gu = mm(window, lane_matrix()).astype(BF)
    gu = gu.reshape(5, GU_WIN, MEMBERS, LANES).transpose(2, 0, 1, 3)
    group = MEMBERS * SPAN
    window = jnp.pad(jnp.where(is_down, rows, 0), ((group, DOWN_WIN * group - CHUNK), (0, 0)))
    window = lax.dynamic_slice_in_dim(window, group - phase_down, DOWN_WIN * group, 0)
    down = window.reshape(DOWN_WIN, MEMBERS, SPAN, LANES).transpose(1, 2, 0, 3)
    return pack_slots(gu, down, chunk)


def pack_slots(gu, down, chunk):
    flat = gu.reshape(MEMBERS, GU_WIN * 5, LANES), down.reshape(MEMBERS, DOWN_WIN * SPAN, LANES)
    plain = jnp.pad(flat[0], ((0, 0), (0, SLOTS - GU_WIN * 5), (0, 0))) + jnp.pad(
        flat[1], ((0, 0), (DOWN_SLOT, SLOTS - DOWN_SLOT - DOWN_WIN * SPAN), (0, 0))
    )
    mixed = jnp.concatenate(
        [
            gu[:, :, :MIX_GU].reshape(MEMBERS, 5 * MIX_GU, LANES),
            down[:, :, MIX_SKIP : MIX_SKIP + 8].reshape(MEMBERS, 8 * SPAN, LANES),
        ],
        axis=1,
    )
    mixed = jnp.pad(mixed, ((0, 0), (0, SLOTS - 5 * MIX_GU - 8 * SPAN), (0, 0)))
    return jnp.where(chunk == DOWN_FIRST, mixed, plain)


def join_chunk(cut, chunk):
    phase, phase_down, is_gu, is_down = chunk_places(chunk)
    gu = cut[:, : GU_WIN * 5].reshape(MEMBERS, 5, GU_WIN, LANES)
    mixed = cut[:, : 5 * MIX_GU].reshape(MEMBERS, 5, MIX_GU, LANES)
    mixed = jnp.pad(mixed, ((0, 0), (0, 0), (0, GU_WIN - MIX_GU), (0, 0)))
    gu = jnp.where(chunk == DOWN_FIRST, mixed, gu)
    gu = gu.transpose(1, 2, 0, 3).reshape(GU_WIN * 5, MEMBERS * LANES)
    gu = mm_nt(gu, lane_matrix())
    gu = gu.reshape(5, GU_WIN, 8, LANES).transpose(1, 0, 2, 3).reshape(GU_WIN, WIDE, LANES)
    gu = gu[:, :TILES].reshape(GU_WIN * TILES, LANES)
    gu = lax.dynamic_slice_in_dim(gu, phase, CHUNK, 0)
    down = cut[:, DOWN_SLOT : DOWN_SLOT + DOWN_WIN * SPAN].reshape(MEMBERS, SPAN, DOWN_WIN, LANES)
    mixed = cut[:, 5 * MIX_GU : 5 * MIX_GU + 8 * SPAN].reshape(MEMBERS, SPAN, 8, LANES)
    mixed = jnp.pad(mixed, ((0, 0), (0, 0), (MIX_SKIP, DOWN_WIN - MIX_SKIP - 8), (0, 0)))
    down = jnp.where(chunk == DOWN_FIRST, mixed, down).transpose(2, 0, 1, 3)
    down = down.reshape(DOWN_WIN * MEMBERS * SPAN, LANES)
    down = lax.dynamic_slice_in_dim(down, phase_down, CHUNK, 0)
    return gu, is_gu, down, is_down


X = ("xl", "xh")


def ring_blocks(block, axis):
    return [block] + [xor(block, axis, step, 4) for step in range(1, 4)]


def ring_gather(block, axis):
    return jnp.stack(ring_blocks(block, axis))


def ring_sum(blocks, axis):
    total = blocks[0].astype(F32)
    for step in range(1, 4):
        total = total + xor(blocks[step], axis, step, 4).astype(F32)
    return total.astype(BF)


def gather_mlp_near(cut):
    low = jnp.broadcast_to(cut[None, :, : SLOTS // 2], (4, MEMBERS, SLOTS // 2, LANES))
    return lax.all_to_all(low, "z", 0, 0, tiled=True), ring_gather(cut[:, SLOTS // 2 :], X)


def gather_mlp_far(low, high):
    return ring_gather(low, X), ring_blocks(high, "z")


def scatter_mlp_far(low, high):
    low = lax.all_to_all(low, "z", 0, 0, tiled=True)
    return jnp.sum(low.astype(F32), axis=0).astype(BF), ring_sum(high, X)


def scatter_mlp_near(low, high):
    return jnp.concatenate([ring_sum(low, X), ring_sum(high, "z")], axis=1)


def chunk_index(chunk):
    return chunk >> 5, ((chunk >> 4) & 1) * 2 + (chunk & 1), (chunk >> 1) & 7


def gu_moves(chunk):
    start = (chunk * CHUNK - GU_START) // TILES
    step = MIX_GU if chunk == DOWN_FIRST else GU_WIN
    moves = []
    for side in range(2):
        low, high = max(0, side * D - start), min(GU_WIN, (side + 1) * D - start)
        for j in range(5 if low < high else 0):
            moves.append((j * step + low, start + low - side * D, high - low, side * UNITS + j * LANES))
    return moves


def down_moves(chunk):
    start = (chunk * CHUNK - DOWN_START) // (MEMBERS * SPAN)
    if chunk == DOWN_FIRST:
        return [(5 * MIX_GU + c * 8, 0, 8, c * LANES) for c in range(SPAN)]
    high = min(DOWN_WIN, UNITS - start)
    return [(DOWN_SLOT + c * DOWN_WIN, start, high, c * LANES) for c in range(SPAN)]


STAGES = 4


def assemble_kernel(here, low, high, gu_w, down_w, stage, gu_sum, down_sum):
    gu_sum[...] = jnp.zeros_like(gu_sum)
    down_sum[...] = jnp.zeros_like(down_sum)
    for chunk in range(GU_FIRST, 128):
        slot = stage.at[chunk % STAGES]
        z, x, member = chunk_index(chunk)
        slot[: SLOTS // 2, :] = low[here[1] ^ x, z, member].astype(F32)
        slot[SLOTS // 2 :, :] = high[here[0] ^ z, here[1] ^ x, member].astype(F32)
        if chunk <= GU_LAST:
            for at, row, count, lane in gu_moves(chunk):
                gu_sum[row : row + count, lane : lane + LANES] += slot[at : at + count, :]
        if chunk >= DOWN_FIRST:
            for at, row, count, lane in down_moves(chunk):
                down_sum[row : row + count, lane : lane + LANES] += slot[at : at + count, :]
    gu_w[...] = gu_sum[...].astype(BF)
    down_w[...] = down_sum[...].astype(BF)


def dissolve(here, gu, down, low, high, stage):
    stage[...] = jnp.zeros_like(stage)
    for chunk in range(128):
        chunk_z, x, member = chunk_index(chunk)
        z, x = here[0] ^ chunk_z, here[1] ^ x
        if chunk < GU_FIRST:
            low[chunk_z, x, member] = jnp.zeros((SLOTS // 2, LANES), BF)
            high[x, z, member] = jnp.zeros((SLOTS // 2, LANES), BF)
            continue
        slot = stage.at[chunk % STAGES]
        if chunk <= GU_LAST:
            for at, row, count, lane in gu_moves(chunk):
                slot[at : at + count, :] = gu[row : row + count, lane : lane + LANES]
        if chunk >= DOWN_FIRST:
            for at, row, count, lane in down_moves(chunk):
                slot[at : at + count, :] = down[row : row + count, lane : lane + LANES]
        low[chunk_z, x, member] = slot[: SLOTS // 2, :].astype(BF)
        high[x, z, member] = slot[SLOTS // 2 :, :].astype(BF)


def vmem(count):
    return [pl.BlockSpec(memory_space=pltpu.VMEM)] * count


def params_of(megabytes):
    return pltpu.CompilerParams(vmem_limit_bytes=megabytes << 20)


def assemble(here, pieces):
    return pl.pallas_call(
        assemble_kernel,
        in_specs=[pl.BlockSpec(memory_space=pltpu.SMEM)] + vmem(2),
        out_specs=vmem(2),
        out_shape=[
            jax.ShapeDtypeStruct((D, 2 * UNITS), BF),
            jax.ShapeDtypeStruct((UNITS, D), BF),
        ],
        scratch_shapes=[
            pltpu.VMEM((STAGES, SLOTS, LANES), F32),
            pltpu.VMEM((D, 2 * UNITS), F32),
            pltpu.VMEM((UNITS, D), F32),
        ],
        compiler_params=params_of(24),
        cost_estimate=pl.CostEstimate(flops=10 << 20, bytes_accessed=20 << 20, transcendentals=0),
        name="assemble",
    )(here, *pieces)


HALF = 8 * CHUNK
ROW_QB = SPAN + Q_ROWS
ROW_K = ROW_QB + SPAN
ROW_KB = ROW_K + D
ROW_V = ROW_KB + 1
ROW_VB = ROW_V + D
ROW_O = ROW_VB + 1
ROW_G2 = ROW_O + Q_ROWS
QKV = D + 2 * LANES


def rotate_tile(tile, cosine, sine):
    half_dim = HEAD_DIM // 2
    lane = lax.broadcasted_iota(jnp.int32, tile.shape, 1)
    other = jnp.where(
        lane % HEAD_DIM < half_dim,
        pltpu.roll(tile, LANES - half_dim, 1),
        pltpu.roll(tile, half_dim, 1),
    )
    return tile * cosine + other * sine


def tile_at(t):
    return slice(t * LANES, (t + 1) * LANES)


def recip_rms(rows):
    return lax.rsqrt(jnp.mean(rows * rows, axis=1, keepdims=True) + EPS)


def norm_back(token_rows, recip, gain, grad_normed):
    scaled = grad_normed * gain
    grad_rows = recip * scaled - token_rows * (recip * recip * recip) * jnp.mean(
        scaled * token_rows, axis=1, keepdims=True
    )
    return grad_rows, jnp.sum(grad_normed * token_rows * recip, axis=0, keepdims=True)


def project_kernel(core, own, other, x, cosine, sine, q, kv, n1, qkv_w, out_w, gain_one, gain_two, rows, qkv_b):
    c = core[0]
    for j in range(8):
        rows[c, j * CHUNK : (j + 1) * CHUNK, :] = own[j].astype(F32)[:CHUNK]
        rows[1 - c, j * CHUNK : (j + 1) * CHUNK, :] = other[j].astype(F32)[:CHUNK]
    for t in range(SPAN):
        lanes = tile_at(t)
        gain_one[:, lanes] = rows[0, t : t + 1, :]
        qkv_w[:, lanes] = rows[0, pl.ds(SPAN + t, D, stride=SPAN), :].astype(BF)
        qkv_b[:, lanes] = rows[0, ROW_QB + t : ROW_QB + t + 1, :]
        out_w[:, lanes] = rows[1, pl.ds(ROW_O - HALF + t, D, stride=SPAN), :].astype(BF)
        gain_two[:, lanes] = rows[1, ROW_G2 - HALF + t : ROW_G2 - HALF + t + 1, :]
    qkv_w[:, tile_at(SPAN)] = rows[0, ROW_K : ROW_K + D, :].astype(BF)
    qkv_b[:, tile_at(SPAN)] = rows[0, ROW_KB : ROW_KB + 1, :]
    near = HALF - ROW_V
    value = jnp.concatenate([rows[0, ROW_V:HALF, :], rows[1, : D - near, :]], axis=0)
    qkv_w[:, tile_at(SPAN + 1)] = value.astype(BF)
    qkv_b[:, tile_at(SPAN + 1)] = rows[1, ROW_VB - HALF : ROW_VB - HALF + 1, :]
    n1[...] = (x[...] * recip_rms(x[...]) * gain_one[...]).astype(BF)
    qkv = mm(n1[...], qkv_w[...]) + qkv_b[...]
    for t in range(SPAN):
        q[:, tile_at(t)] = rotate_tile(qkv[:, tile_at(t)], cosine[...], sine[...]).astype(BF)
    kv[:, :LANES] = rotate_tile(qkv[:, tile_at(SPAN)], cosine[...], sine[...]).astype(BF)
    kv[:, LANES:] = qkv[:, tile_at(SPAN + 1)].astype(BF)


def project(core, own, other, x, cosine, sine):
    tokens = x.shape[0]
    return pl.pallas_call(
        project_kernel,
        in_specs=[pl.BlockSpec(memory_space=pltpu.SMEM)] + vmem(5),
        out_specs=vmem(7),
        out_shape=[
            jax.ShapeDtypeStruct((tokens, D), BF),
            jax.ShapeDtypeStruct((tokens, 2 * LANES), BF),
            jax.ShapeDtypeStruct((tokens, D), BF),
            jax.ShapeDtypeStruct((D, QKV), BF),
            jax.ShapeDtypeStruct((D, D), BF),
            jax.ShapeDtypeStruct((1, D), F32),
            jax.ShapeDtypeStruct((1, D), F32),
        ],
        scratch_shapes=[pltpu.VMEM((2, HALF, LANES), F32), pltpu.VMEM((1, QKV), F32)],
        compiler_params=params_of(24),
        cost_estimate=pl.CostEstimate(flops=300 << 20, bytes_accessed=20 << 20, transcendentals=0),
        name="project",
    )(core, own, other, x, cosine, sine)


def pack_kernel(
    core, dqp, n1, x, qkv_w, gain_one, attended, grad_attn, grad_mid, gain_two, cosine, sine, dkv,
    input_grad, mine, theirs, rows, dqkv,
):
    c = core[0]
    total = dkv[0].astype(F32)
    for j in range(1, 8):
        total = total + dkv[j].astype(F32)
    dqkv[:, :D] = dqp[...]
    dqkv[:, tile_at(SPAN)] = rotate_tile(total[:, :LANES], cosine[...], -sine[...]).astype(BF)
    dqkv[:, tile_at(SPAN + 1)] = total[:, LANES:].astype(BF)
    grad_n1 = mm_nt(dqkv[...], qkv_w[...])
    recip = recip_rms(x[...])
    grad_rows, grad_gain = norm_back(x[...], recip, gain_one[...], grad_n1)
    input_grad[...] = grad_mid[...] + grad_rows
    grad = mm_tn(n1[...], dqkv[...])
    bias = jnp.sum(dqkv[...].astype(F32), axis=0, keepdims=True)
    grad_out = mm_tn(attended[...], grad_attn[...])
    for t in range(SPAN):
        lanes = tile_at(t)
        rows[0, t : t + 1, :] = grad_gain[:, lanes]
        rows[0, pl.ds(SPAN + t, D, stride=SPAN), :] = grad[:, lanes]
        rows[0, ROW_QB + t : ROW_QB + t + 1, :] = bias[:, lanes]
        rows[1, pl.ds(ROW_O - HALF + t, D, stride=SPAN), :] = grad_out[:, lanes]
        rows[1, ROW_G2 - HALF + t : ROW_G2 - HALF + t + 1, :] = gain_two[:, lanes]
    rows[0, ROW_K : ROW_K + D, :] = grad[:, tile_at(SPAN)]
    rows[0, ROW_KB : ROW_KB + 1, :] = bias[:, tile_at(SPAN)]
    near = HALF - ROW_V
    rows[0, ROW_V:HALF, :] = grad[:near, tile_at(SPAN + 1)]
    rows[1, : D - near, :] = grad[near:, tile_at(SPAN + 1)]
    rows[1, ROW_VB - HALF : ROW_VB - HALF + 1, :] = bias[:, tile_at(SPAN + 1)]
    rows[1, GU_START - HALF :, :] = jnp.zeros((2 * HALF - GU_START, LANES), F32)
    tail = jnp.zeros((PARTS * PART_ROWS - CHUNK, LANES), F32)
    for j in range(8):
        mine[j] = jnp.concatenate([rows[c, j * CHUNK : (j + 1) * CHUNK, :], tail]).astype(BF)
        theirs[j] = jnp.concatenate([rows[1 - c, j * CHUNK : (j + 1) * CHUNK, :], tail]).astype(BF)


def pack(core, *arrays):
    tokens = arrays[1].shape[0]
    return pl.pallas_call(
        pack_kernel,
        in_specs=[pl.BlockSpec(memory_space=pltpu.SMEM)] + vmem(len(arrays)),
        out_specs=vmem(3),
        out_shape=[
            jax.ShapeDtypeStruct((tokens, D), F32),
            jax.ShapeDtypeStruct((8, PARTS * PART_ROWS, LANES), BF),
            jax.ShapeDtypeStruct((8, PARTS * PART_ROWS, LANES), BF),
        ],
        scratch_shapes=[pltpu.VMEM((2, HALF, LANES), F32), pltpu.VMEM((tokens, QKV), BF)],
        compiler_params=params_of(24),
        cost_estimate=pl.CostEstimate(flops=800 << 20, bytes_accessed=20 << 20, transcendentals=0),
        name="pack",
    )(core, *arrays)


def place_heads(blocks, k_at, v_at):
    kv = blocks[...].reshape(-1, 2 * LANES)
    for source, target in ((kv[:, :LANES], k_at), (kv[:, LANES:], v_at)):
        wide = source.astype(F32)
        low = lax.broadcasted_iota(jnp.int32, wide.shape, 1) < HEAD_DIM
        first, second = jnp.where(low, wide, 0.0), jnp.where(low, 0.0, wide)
        target[0] = first.astype(BF)
        target[1] = pltpu.roll(first, HEAD_DIM, 1).astype(BF)
        target[2] = pltpu.roll(second, HEAD_DIM, 1).astype(BF)
        target[3] = second.astype(BF)


def mark_keys(seg_q, seg_k, place_q, place_k, keep):
    allowed = (seg_q[...] == seg_k[...]) & (place_k[...] <= place_q[...])
    keep[...] = jnp.where(allowed, 1.0, 0.0)


def attend_kernel(
    q, kv, seg_q, seg_k, place_q, place_k, x, out_w, gain_two, attended, lse, mid, n2, k_at, v_at, keep
):
    place_heads(kv, k_at, v_at)
    mark_keys(seg_q, seg_k, place_q, place_k, keep)
    for t in range(SPAN):
        total_out = None
        for half in range(2):
            head = 2 * t + half
            at = (head // GROUP) * 2 + half
            scores = mm_nt(q[:, tile_at(t)], k_at[at]) * (HEAD_DIM**-0.5)
            scores = jnp.where(keep[...] > 0.0, scores, -1e30)
            peak = jnp.max(scores, axis=1, keepdims=True)
            raised = jnp.exp(scores - peak)
            total = jnp.sum(raised, axis=1, keepdims=True)
            shares = (raised * (1.0 / total)).astype(BF)
            part = mm(shares, v_at[at])
            total_out = part if total_out is None else total_out + part
            lse[:, head : head + 1] = peak + jnp.log(total)
        attended[:, tile_at(t)] = total_out.astype(BF)
    mid[...] = x[...] + mm(attended[...], out_w[...])
    n2[...] = (mid[...] * recip_rms(mid[...]) * gain_two[...]).astype(BF)


def attend_back_kernel(
    g0, g1, g2, g3, mid, gain_two, grad_out, out_w, q, kv, lse, seg_q, seg_k, place_q, place_k, cosine, sine,
    grad_mid, grad_attn, dqp, grad_gain, dkv, k_at, v_at, keep, sums,
):
    grad_n2 = g0[...] + g1[...].astype(F32) + g2[...].astype(F32) + g3[...].astype(F32)
    recip = recip_rms(mid[...])
    grad_rows, gain = norm_back(mid[...], recip, gain_two[...], grad_n2)
    grad_gain[...] = gain
    grad_mid[...] = grad_out[...] + grad_rows
    grad_attn[...] = grad_mid[...].astype(BF)
    do = mm_nt(grad_attn[...], out_w[...]).astype(BF)
    place_heads(kv, k_at, v_at)
    mark_keys(seg_q, seg_k, place_q, place_k, keep)
    sums[...] = jnp.zeros_like(sums)
    scale = HEAD_DIM**-0.5
    for t in range(SPAN):
        q_tile, do_tile = q[:, tile_at(t)], do[:, tile_at(t)]
        grad_q = None
        for half in range(2):
            head = 2 * t + half
            group = head // GROUP
            at = group * 2 + half
            scores = mm_nt(q_tile, k_at[at]) * scale
            scores = jnp.where(keep[...] > 0.0, scores, -1e30)
            shares = jnp.exp(scores - lse[:, head : head + 1])
            grad_shares = mm_nt(do_tile, v_at[at])
            delta = jnp.sum(shares * grad_shares, axis=1, keepdims=True)
            grad_scores = (shares * (grad_shares - delta)).astype(BF)
            part = mm(grad_scores, k_at[at])
            grad_q = part if grad_q is None else grad_q + part
            mine = slice(half * HEAD_DIM, (half + 1) * HEAD_DIM)
            sums[group * HEAD_DIM : (group + 1) * HEAD_DIM, :] += mm_tn(q_tile, grad_scores)[mine]
            sums[LANES + group * HEAD_DIM : LANES + (group + 1) * HEAD_DIM, :] += mm_tn(
                do_tile, shares.astype(BF)
            )[mine]
        dqp[:, tile_at(t)] = rotate_tile(grad_q * scale, cosine[...], -sine[...]).astype(BF)
    for j in range(8):
        dkv[j, :, :LANES] = (jnp.transpose(sums[:LANES, tile_at(j)]) * scale).astype(BF)
        dkv[j, :, LANES:] = jnp.transpose(sums[LANES:, tile_at(j)]).astype(BF)


def head_scratch(tokens, length):
    return [
        pltpu.VMEM((4, length, LANES), BF),
        pltpu.VMEM((4, length, LANES), BF),
        pltpu.VMEM((tokens, length), F32),
    ]


def attend(q, kv, masks, x, out_w, gain_two):
    tokens, length = q.shape[0], masks[1].shape[1]
    return pl.pallas_call(
        attend_kernel,
        in_specs=vmem(9),
        out_specs=vmem(4),
        out_shape=[
            jax.ShapeDtypeStruct((tokens, D), BF),
            jax.ShapeDtypeStruct((tokens, 16), F32),
            jax.ShapeDtypeStruct((tokens, D), F32),
            jax.ShapeDtypeStruct((tokens, D), BF),
        ],
        scratch_shapes=head_scratch(tokens, length),
        compiler_params=params_of(24),
        cost_estimate=pl.CostEstimate(
            flops=8 * HEADS * tokens * length * HEAD_DIM,
            bytes_accessed=4 << 20,
            transcendentals=HEADS * tokens * length,
        ),
        name="attend",
    )(q, kv, *masks, x, out_w, gain_two)


def attend_back(grads, mid, gain_two, grad_out, out_w, q, kv, lse, masks, cosine, sine):
    tokens, length = q.shape[0], masks[1].shape[1]
    return pl.pallas_call(
        attend_back_kernel,
        in_specs=vmem(17),
        out_specs=vmem(5),
        out_shape=[
            jax.ShapeDtypeStruct((tokens, D), F32),
            jax.ShapeDtypeStruct((tokens, D), BF),
            jax.ShapeDtypeStruct((tokens, D), BF),
            jax.ShapeDtypeStruct((1, D), F32),
            jax.ShapeDtypeStruct((8, tokens, 2 * LANES), BF),
        ],
        scratch_shapes=head_scratch(tokens, length) + [pltpu.VMEM((2 * LANES, length), F32)],
        compiler_params=params_of(24),
        cost_estimate=pl.CostEstimate(
            flops=20 * HEADS * tokens * length * HEAD_DIM,
            bytes_accessed=8 << 20,
            transcendentals=HEADS * tokens * length,
        ),
        name="attend_back",
    )(*grads, mid, gain_two, grad_out, out_w, q, kv, lse, *masks, cosine, sine)


def mlp_kernel(
    here, x_near, x_far, dy_near, dy_far, gu_w, down_w,
    y_near, y_far, dx_near, dx_far, low, high, sum_gu, sum_down, stage,
):
    halves = (x_near, dy_near, y_near, dx_near), (x_far, dy_far, y_far, dx_far)
    for first, (x_ref, dy_ref, y_ref, dx_ref) in zip((True, False), halves):
        x, dy = x_ref[...], dy_ref[...]
        both = mm(x, gu_w[...])
        gate, up = both[:, :UNITS], both[:, UNITS:]
        dh = mm_nt(dy, down_w[...])
        sigmoid = 1.0 / (1.0 + jnp.exp(-gate))
        silu = gate * sigmoid
        hidden = (silu * up).astype(BF)
        dg = (dh * up * sigmoid * (1.0 + gate * (1.0 - sigmoid))).astype(BF)
        du = (dh * silu).astype(BF)
        y_ref[...] = mm(hidden, down_w[...]).astype(BF)
        both = jnp.concatenate([dg, du], axis=1)
        dx_ref[...] = mm_nt(both, gu_w[...]).astype(BF)
        if first:
            sum_gu[...] = mm_tn(x, both)
            sum_down[...] = mm_tn(hidden, dy)
        else:
            sum_gu[...] += mm_tn(x, both)
            sum_down[...] += mm_tn(hidden, dy)
    dissolve(here, sum_gu, sum_down, low, high, stage)


def feed_forward(here, x, dy, gu_w, down_w):
    tokens = x[0].shape[0]
    sides = jax.ShapeDtypeStruct((tokens, D), BF)
    return pl.pallas_call(
        mlp_kernel,
        in_specs=[pl.BlockSpec(memory_space=pltpu.SMEM)] + vmem(6),
        out_specs=vmem(6),
        out_shape=[
            sides,
            sides,
            sides,
            sides,
            jax.ShapeDtypeStruct((4, 4, MEMBERS, SLOTS // 2, LANES), BF),
            jax.ShapeDtypeStruct((4, 4, MEMBERS, SLOTS // 2, LANES), BF),
        ],
        scratch_shapes=[
            pltpu.VMEM((D, 2 * UNITS), F32),
            pltpu.VMEM((UNITS, D), F32),
            pltpu.VMEM((STAGES, SLOTS, LANES), F32),
        ],
        compiler_params=params_of(30),
        cost_estimate=pl.CostEstimate(
            flops=36 * tokens * D * UNITS, bytes_accessed=16 << 20, transcendentals=2 * tokens * UNITS
        ),
        name="feed_forward",
    )(here, *x, *dy, gu_w, down_w)


def rope_tables(positions):
    half_dim = HEAD_DIM // 2
    freqs = ROPE_BASE ** (-(jnp.arange(half_dim, dtype=F32) * 2.0) / HEAD_DIM)
    angles = positions.astype(F32)[:, None] * freqs
    cosine, sine = jnp.cos(angles), jnp.sin(angles)
    return jnp.concatenate([cosine] * 4, axis=1), jnp.concatenate([-sine, sine] * 2, axis=1)


def spread_near(block):
    return jnp.concatenate([block] + [xor(block, "y", step, 4) for step in range(1, 4)])


def spread(block):
    near = spread_near(block)
    return near, swap(near, "c")


def collect_far(near, far):
    return (near.astype(F32) + swap(far, "c").astype(F32)).reshape(4, -1, D)


def collect_near(total):
    return [total[0]] + [xor(total[step].astype(BF), "y", step, 4) for step in range(1, 4)]


def local(inputs, params, segments, cotangent):
    tokens = inputs.shape[1]
    length = segments.shape[1]
    x = inputs[0]
    grad_out = cotangent[0]
    chunk = lax.axis_index(("z", "xl", "c", "y", "xh"))
    place = lax.axis_index(("y", "xh"))
    core = lax.axis_index("c").astype(jnp.int32).reshape(1)
    here = jnp.stack([lax.axis_index("z"), lax.axis_index(X)]).astype(jnp.int32)

    seg_row = segments[0]
    place_mine = place * tokens + jnp.arange(tokens, dtype=jnp.int32)
    seg_mine = lax.dynamic_slice_in_dim(seg_row, place * tokens, tokens, 0)
    place_keys = jnp.arange(length, dtype=jnp.int32)
    masks = (seg_mine[:, None], seg_row[None, :], place_mine[:, None], place_keys[None, :])
    doc_start = jnp.sum((seg_row[None, :] < seg_mine[:, None]).astype(jnp.int32), axis=1)
    cosine, sine = rope_tables(place_mine - doc_start)

    rows = params.reshape(CHUNK, LANES).astype(BF)
    part = scatter_rows(rows)
    cut = lax.all_to_all(cut_chunk(rows, chunk), ("c", "y"), 0, 0, tiled=True)
    pieces = gather_mlp_near(cut)
    dy = spread(grad_out.astype(BF))
    part, pieces, dy, cosine, sine = lax.optimization_barrier((part, pieces, dy, cosine, sine))
    own = gather_rows(part)
    other = swap(own, "c")
    low, high = gather_mlp_far(*pieces)

    q, kv, normed_one, qkv_w, out_w, gain_one, gain_two = project(core, own, other, x, cosine, sine)
    kv = lax.all_to_all(jnp.broadcast_to(kv[None], (8,) + kv.shape), ("y", "xh"), 0, 0, tiled=True)
    kv, high = lax.optimization_barrier((kv, high))
    attended, lse, mid, normed_two = attend(q, kv, masks, x, out_w, gain_two)
    near, low = lax.optimization_barrier((spread_near(normed_two), low))
    n2 = near, swap(near, "c")
    gu_w, down_w = assemble(here, (low, jnp.stack(high)))
    y_near, y_far, dx_near, dx_far, low, high = feed_forward(here, n2, dy, gu_w, down_w)
    grads, high = lax.optimization_barrier((collect_far(dx_near, dx_far), high))
    grads = collect_near(grads)
    low, high = scatter_mlp_far(low, high)
    grad_mid, grad_attn, dqp, grad_gain_two, dkv = attend_back(
        grads, mid, gain_two, grad_out, out_w, q, kv, lse, masks, cosine, sine
    )
    dkv, y_near, y_far = lax.optimization_barrier((dkv, y_near, y_far))
    dkv = lax.all_to_all(dkv, ("y", "xh"), 0, 0, tiled=True)
    dkv, mlp_part = lax.optimization_barrier((dkv, scatter_mlp_near(low, high)))
    input_grad, mine, theirs = pack(
        core, dqp, normed_one, x, qkv_w, gain_one, attended, grad_attn, grad_mid, grad_gain_two, cosine, sine, dkv
    )
    mlp_grads = lax.all_to_all(mlp_part, ("c", "y"), 0, 0, tiled=True)
    attn_mine = gather_rows_sum(scatter_rows_sum(mine, theirs))
    terms = collect_near(collect_far(y_near, y_far))
    outputs = mid + terms[0] + terms[1].astype(F32) + terms[2].astype(F32) + terms[3].astype(F32)

    gu_mine, is_gu, down_mine, is_down = join_chunk(mlp_grads, chunk)
    flat_row = chunk * CHUNK + jnp.arange(CHUNK, dtype=jnp.int32)[:, None]
    param_grad = jnp.where(flat_row < GU_START, attn_mine, 0.0)
    param_grad = jnp.where(is_gu, gu_mine, param_grad)
    param_grad = jnp.where(is_down, down_mine.astype(F32), param_grad)
    return outputs[None], input_grad[None], param_grad.reshape(-1)


def solution(mesh):
    fine = Mesh(mesh.devices.reshape(4, 2, 2, 4, 2), ("z", "xl", "c", "y", "xh"))
    dp, seq = ("z", "xl", "c"), ("y", "xh")
    placed = (P(dp, seq, None), P(dp + seq), P(dp, None), P(dp, seq, None))
    return jax.shard_map(
        local,
        mesh=fine,
        in_specs=placed,
        out_specs=(P(dp, seq, None), P(dp, seq, None), P(dp + seq)),
        check_vma=False,
    )
```
